32 devices in a mesh: tr: 8 (over z, x), tc: 4 (over y, core).
Axes of the slice: x: 2, y: 2, z: 4, core: 2. Of those that a mesh axis runs over, the one named last changes fastest.
Arguments:
- frame_one: bfloat16 [16, 256, 128], P('tr', 'tc'), may hold values from -20 to 20
- frame_two: bfloat16 [16, 256, 128], P('tr', 'tc'), may hold values from -20 to 20
- first_kernel: bfloat16 [3, 3, 128, 128], replicated, may hold values from -0.1875 to 0.1875
- second_kernel: bfloat16 [3, 3, 128, 128], replicated, may hold values from -0.1875 to 0.1875
- out_proj: bfloat16 [128, 256], replicated, may hold values from -0.5 to 0.5
- out_bias: float32 [256], replicated, may hold values from -0.4 to 0.4
Outputs:
- corr_level1: bfloat16 [16, 256, 1024], P('tr', 'tc')
- corr_level2: bfloat16 [16, 256, 256], P('tr', 'tc')
- corr_level3: bfloat16 [16, 256, 64], P('tr', 'tc')
The draws below stay inside these ranges and needn't reach their ends.
All inputs are finite; a program needn't handle non-finite values.
Results may differ from the reference program's by a relative error of at most 0.0035.
Values may be sent and summed in bfloat16 or wider, within the bound.
A program may use at most 64 MiB of HBM per device.

```python
import jax
import jax.numpy as jnp
from jax import lax

CIN = 128
CH = 256
HEIGHT = 16
WIDTH = 256


def frame_values(key, salt):
    key = jax.random.fold_in(key, salt)
    noise_key, channel_key, offset_key = jax.random.split(key, 3)
    extent = (HEIGHT, WIDTH, CIN)
    heights = jnp.arange(HEIGHT, dtype=jnp.float32) / float(max(HEIGHT - 1, 1))
    channel = jnp.exp(jax.random.uniform(channel_key, (CIN,), jnp.float32, jnp.log(0.3), jnp.log(3.0)))
    offset = jax.random.uniform(offset_key, (CIN,), jnp.float32, -0.5, 0.5)
    random_part = jnp.clip(jax.random.normal(noise_key, extent, jnp.float32), -4.0, 4.0)
    rising = 0.5 * 3.0 ** heights
    values = random_part * rising[:, None, None] * channel + offset
    return values.astype(jnp.bfloat16)


def draw_frame_one(key, part):
    return frame_values(key, 11)


def draw_frame_two(key, part):
    return frame_values(key, 23)


def noise(own_key, shape, width, reach, kind=jnp.bfloat16):
    values = width * jax.random.normal(own_key, shape, jnp.float32)
    return jnp.clip(values, min=-reach, max=reach).astype(kind)


def setup_inputs(seed: int = 0) -> dict:
    seeds = jax.random.split(jax.random.key(seed), 7)
    return {
        "frame_one": draw_frame_one(jax.random.fold_in(seeds[6], 71), 0),
        "frame_two": draw_frame_two(jax.random.fold_in(seeds[6], 71), 0),
        "first_kernel": noise(seeds[2], (3, 3, CIN, CIN), (9 * CIN) ** -0.5, 0.1875),
        "second_kernel": noise(seeds[3], (3, 3, CIN, CIN), (9 * CIN) ** -0.5, 0.1875),
        "out_proj": noise(seeds[4], (CIN, CH), CIN ** -0.5, 0.5),
        "out_bias": jnp.clip(jax.random.uniform(seeds[5], (CH,), jnp.float32, -0.4, 0.4), -0.4, 0.4),
    }


def convolve(padded, kernel):
    out_rows = padded.shape[1] - 2
    out_cols = padded.shape[2] - 2
    summed = jnp.zeros((padded.shape[0], out_rows, out_cols, kernel.shape[3]), jnp.float32)
    for down_step in range(3):
        for side_step in range(3):
            window = padded[:, down_step:down_step + out_rows, side_step:side_step + out_cols, :].astype(jnp.float32)
            summed = summed + jnp.einsum('fhwc,cd->fhwd', window, kernel[down_step, side_step].astype(jnp.float32), precision=lax.Precision.HIGHEST)
    return summed

def normalize(values, positions):
    centre = lax.optimization_barrier(jnp.sum(values, axis=(1, 2))) / positions
    spread = lax.optimization_barrier(jnp.sum(values * values, axis=(1, 2))) / positions - centre * centre
    inverse = lax.rsqrt(spread + 1e-05)
    return jax.nn.relu((values - centre[:, None, None, :]) * inverse[:, None, None, :])

def pad_grid(values):
    return jnp.pad(values, ((0, 0), (1, 1), (1, 1), (0, 0)))

def reference(frame_one, frame_two, first_kernel, second_kernel, out_proj, out_bias):
    frames = jnp.stack([frame_one, frame_two])
    height = frames.shape[1]
    widths = frames.shape[2]
    positions = float(height * widths)
    first = convolve(pad_grid(frames), first_kernel)
    hidden = normalize(first, positions).astype(jnp.bfloat16)
    second = convolve(pad_grid(hidden), second_kernel)
    blocks = jax.nn.relu(frames.astype(jnp.float32) + normalize(second, positions)).astype(jnp.bfloat16)
    feature = (jnp.einsum('fhwc,cd->fhwd', blocks.astype(jnp.float32), out_proj.astype(jnp.float32), precision=lax.Precision.HIGHEST) + out_bias).astype(jnp.bfloat16)
    channels = feature.shape[3]
    query_rows = feature[0].astype(jnp.float32)
    key_matrix = feature[1].astype(jnp.float32).reshape(height * widths, channels)
    inv_root = 1.0 / jnp.sqrt(jnp.float32(channels))

    def one_row(row_queries):
        matches = jnp.dot(row_queries, key_matrix.T, precision=lax.Precision.HIGHEST, preferred_element_type=jnp.float32) * inv_root
        matches = matches.reshape(widths, height, widths)
        results = []
        for level_index in (1, 2, 3):
            factor = 2 ** level_index
            pooled = lax.optimization_barrier(jnp.sum(matches.reshape(widths, height // factor, factor, widths // factor, factor), axis=(2, 4))) / float(factor * factor)
            results.append(pooled.reshape(widths, -1).astype(jnp.bfloat16))
        return tuple(results)
    level_one, level_two, level_three = lax.map(one_row, query_rows)
    return (level_one, level_two, level_three)
```

```python
import functools
import math

import jax
import jax.numpy as jnp
from jax import lax
from jax.experimental import pallas as pl
from jax.experimental.pallas import tpu as pltpu
from jax.sharding import PartitionSpec as P

MESH = pl.DeviceIdType.MESH
F32 = jnp.float32
BF16 = jnp.bfloat16


def dot_t(a, b):
    return lax.dot_general(a, b, (((1,), (1,)), ((), ())), preferred_element_type=F32)


def split(values):
    high = values.astype(BF16)
    low = (values - high.astype(F32)).astype(BF16)
    return high, low


def kernel(
    row_tiles, col_tiles, rows, cols,
    f1, f2, w1_hbm, w2_hbm, wp_hbm, bias_hbm,
    o1, o2, o3,
    w1, w2, wp, bias,
    tiles, edge_rows, edge_out, edge_in,
    grid, patches, conv_own, conv_edge, hidden, patches2,
    stat_one, stat_two, keys, pool_a, pool_b, pool_c,
    in_sem, row_send, row_recv, edge_send, edge_recv, all_send, all_recv,
):
    tr = lax.axis_index("tr")
    tc = lax.axis_index("tc")
    devices = row_tiles * col_tiles
    me = tr * col_tiles + tc
    positions = float(devices * rows * cols)
    channels = wp.shape[1]
    pooled_cols = cols // 2

    loads = [
        pltpu.make_async_copy(f1, tiles.at[0], in_sem.at[0]),
        pltpu.make_async_copy(f2, tiles.at[1], in_sem.at[1]),
        pltpu.make_async_copy(w1_hbm, w1, in_sem.at[2]),
        pltpu.make_async_copy(w2_hbm, w2, in_sem.at[3]),
        pltpu.make_async_copy(wp_hbm, wp, in_sem.at[4]),
        pltpu.make_async_copy(bias_hbm, bias, in_sem.at[5]),
    ]
    for load in loads:
        load.start()

    edge_rows[...] = jnp.zeros_like(edge_rows)
    edge_in[...] = jnp.zeros_like(edge_in)

    def place_of(index):
        return (index // col_tiles, lax.rem(index, col_tiles))

    barrier = pltpu.get_barrier_semaphore()

    def greet(step, carried):
        other = lax.rem(me + step, devices)
        pl.semaphore_signal(barrier, inc=1, device_id=place_of(other), device_id_type=MESH)
        return carried

    lax.fori_loop(1, devices, greet, 0)

    loads[0].wait()
    loads[1].wait()
    left = 16
    right = left + cols
    for f in range(2):
        for y in range(2):
            values = tiles[f, y].astype(F32)
            grid[f, 2 + y, left:right, :] = values
            line = f * 4 + y * 2
            edge_out[0, line:line + 2, :] = values[0:2]
            edge_out[1, line:line + 2, :] = values[cols - 2:cols]

    pl.semaphore_wait(barrier, devices - 1)

    def inside(down, side):
        row = tr + down
        col = tc + side
        return (row >= 0) & (row < row_tiles) & (col >= 0) & (col < col_tiles)

    corners = [
        (0, 1, 1, 0), (0, -1, 0, 1),
        (1, 1, 1, 2), (1, -1, 0, 3),
        (-1, 1, 1, 4), (-1, -1, 0, 5),
    ]
    lines = [(1, 1, 0), (-1, 0, 1), (1, 0, 2), (-1, 1, 3)]

    def row_copies(down, row, slot):
        return [
            pltpu.make_async_remote_copy(
                src_ref=frame.at[row], dst_ref=edge_rows.at[slot, f],
                send_sem=row_send.at[slot], recv_sem=row_recv.at[slot],
                device_id=(tr + down, tc), device_id_type=MESH,
            )
            for f, frame in enumerate((f1, f2))
        ]

    def edge_copy(down, side, which, slot):
        return pltpu.make_async_remote_copy(
            src_ref=edge_out.at[which], dst_ref=edge_in.at[slot],
            send_sem=edge_send.at[slot], recv_sem=edge_recv.at[slot],
            device_id=(tr + down, tc + side), device_id_type=MESH,
        )

    def send_row(line):
        @pl.when(inside(line[0], 0))
        def _():
            for copy in row_copies(*line):
                copy.start()

    def send_edge(corner):
        @pl.when(inside(corner[0], corner[1]))
        def _():
            edge_copy(*corner).start()

    def await_row(line):
        slot = line[2]

        @pl.when(inside(-line[0], 0))
        def _():
            pltpu.make_async_copy(edge_rows.at[slot], edge_rows.at[slot], row_recv.at[slot]).wait()

    def await_edge(corner):
        slot = corner[3]

        @pl.when(inside(-corner[0], -corner[1]))
        def _():
            pltpu.make_async_copy(edge_in.at[slot], edge_in.at[slot], edge_recv.at[slot]).wait()

    for line in lines[:2]:
        send_row(line)
    for corner in corners:
        send_edge(corner)
    for line in lines[2:]:
        send_row(line)

    def fill_row(y, slot):
        for f in range(2):
            grid[f, y, left:right, :] = edge_rows[slot, f].astype(F32)

    def fill_edges(y, slot, base):
        for f in range(2):
            line = f * 4 + base * 2
            grid[f, y, left - 2:left, :] = edge_in[slot, line:line + 2, :]
            grid[f, y, right:right + 2, :] = edge_in[slot + 1, line:line + 2, :]

    wide = cols + 16

    def fill_patches(y):
        for f in range(2):
            for j in range(3):
                start = left - 9 + j
                patches[f, y, :, j * 128:(j + 1) * 128] = grid[f, y, start:start + wide, :].astype(BF16)

    for line in lines[:2]:
        await_row(line)
    for corner in corners:
        await_edge(corner)
    fill_row(1, 0)
    fill_row(4, 1)
    for y in range(2):
        fill_edges(2 + y, 0, y)
        fill_edges(0 + y, 2, y)
        fill_edges(4 + y, 4, y)
    for y in range(1, 5):
        fill_patches(y)

    loads[2].wait()

    def convolve(first_row, count):
        total = None
        for i in range(3):
            window = patches[:, first_row - 1 + i:first_row - 1 + i + count]
            part = jnp.dot(window.reshape(2 * count * wide, 384), w1[i], preferred_element_type=F32)
            total = part if total is None else total + part
        return total.reshape(2, count, wide, 128)

    def share(stats, slots, phase):
        slots[me] = stats

        def give(step, carried):
            other = lax.rem(me + step, devices)
            pltpu.make_async_remote_copy(
                src_ref=slots.at[me], dst_ref=slots.at[me],
                send_sem=all_send.at[phase], recv_sem=all_recv.at[phase],
                device_id=place_of(other), device_id_type=MESH,
            ).start()
            return carried

        lax.fori_loop(1, devices, give, 0)

    def sums_of(values):
        total = jnp.sum(values, axis=(1, 2))
        squares = jnp.sum(values * values, axis=(1, 2))
        return jnp.concatenate([total, squares], axis=0)

    def collect(slots, phase):
        others = slots.at[pl.ds(0, devices - 1)]
        pltpu.make_async_copy(others, others, all_recv.at[phase]).wait()
        total = jnp.sum(slots[...], axis=0) / positions
        centre = total[0:2]
        spread = total[2:4] - centre * centre
        return centre[:, None, None, :], lax.rsqrt(spread + 1e-05)[:, None, None, :]

    own = convolve(2, 2)
    conv_own[...] = own
    share(sums_of(own[:, :, 8:8 + cols]), stat_one, 0)

    for line in lines[2:]:
        await_row(line)
    fill_row(0, 2)
    fill_row(5, 3)
    fill_patches(0)
    fill_patches(5)
    conv_edge[:, 0:1] = convolve(1, 1)
    conv_edge[:, 1:2] = convolve(4, 1)
    loads[3].wait()

    centre, inverse = collect(stat_one, 0)
    spot = lax.broadcasted_iota(jnp.int32, (1, 1, wide, 128), 2)
    col_ok = ((spot >= 8) | (tc > 0)) & ((spot < 8 + cols) | (tc < col_tiles - 1))

    def normal(values, keep):
        return jnp.where(keep, jax.nn.relu((values - centre) * inverse), 0.0)

    hidden[:, 1:3, 8:8 + wide, :] = normal(conv_own[...], col_ok)
    hidden[:, 0:1, 8:8 + wide, :] = normal(conv_edge[:, 0:1], col_ok & (tr > 0))
    hidden[:, 3:4, 8:8 + wide, :] = normal(conv_edge[:, 1:2], col_ok & (tr < row_tiles - 1))
    for f in range(2):
        for y in range(4):
            for j in range(3):
                start = left - 1 + j
                patches2[f, y, :, j * 128:(j + 1) * 128] = hidden[f, y, start:start + cols, :].astype(BF16)
    second = None
    for i in range(3):
        window = patches2[:, i:i + 2].reshape(4 * cols, 384)
        part = jnp.dot(window, w2[i], preferred_element_type=F32)
        second = part if second is None else second + part
    second = second.reshape(2, 2, cols, 128)
    share(sums_of(second), stat_two, 1)
    loads[4].wait()
    loads[5].wait()
    centre, inverse = collect(stat_two, 1)
    blocks = jax.nn.relu(tiles[...].astype(F32) + jax.nn.relu((second - centre) * inverse)).astype(BF16)

    pool_a[0:cols, :] = blocks[1, 0].astype(F32) + blocks[1, 1].astype(F32)
    small = (pool_a[pl.ds(0, pooled_cols, stride=2), :] + pool_a[pl.ds(1, pooled_cols, stride=2), :]) * 0.25
    mine = pl.ds(pl.multiple_of(me * pooled_cols, pooled_cols), pooled_cols)
    keys[mine, :] = small.astype(BF16)

    def give_keys(step, carried):
        other = lax.rem(me + step, devices)
        pltpu.make_async_remote_copy(
            src_ref=keys.at[mine], dst_ref=keys.at[mine],
            send_sem=all_send.at[2], recv_sem=all_recv.at[2],
            device_id=place_of(other), device_id_type=MESH,
        ).start()
        return carried

    lax.fori_loop(1, devices, give_keys, 0)

    scale = 1.0 / math.sqrt(channels)
    feature = jnp.dot(blocks[0].reshape(2 * cols, 128), wp[...], preferred_element_type=F32) + bias[...]
    feature = feature.astype(BF16)
    offset = jnp.sum(feature.astype(F32) * bias[...], axis=1, keepdims=True) * scale
    high, low = split(dot_t(feature, wp[...]) * scale)
    queries = jnp.concatenate([high, low], axis=1)

    others = keys.at[pl.ds(0, (devices - 1) * pooled_cols)]
    pltpu.make_async_copy(others, others, all_recv.at[2]).wait()

    across = col_tiles * pooled_cols
    total_keys = devices * pooled_cols
    chunk = min(total_keys, 2048)
    lines1 = chunk // across

    def pooled(values, scratch, lines_in, width):
        pairs = jnp.sum(values.reshape(lines_in // 2, 2, width, 128), axis=1)
        count = lines_in // 2 * width
        scratch[0:count, :] = pairs.reshape(count, 128)
        half = count // 2
        return (scratch[pl.ds(0, half, stride=2), :] + scratch[pl.ds(1, half, stride=2), :]) * 0.25

    def fine(values):
        k_high, k_low = split(values)
        return dot_t(queries, jnp.concatenate([k_high, k_high], axis=1)) + dot_t(high, k_low) + offset

    for start in range(0, total_keys, chunk):
        part = keys[start:start + chunk, :]
        level = dot_t(queries, jnp.concatenate([part, part], axis=1)) + offset
        o1[:, start:start + chunk] = level.astype(BF16)
        two = pooled(part.astype(F32), pool_b, lines1, across)
        o2[:, start // 4:(start + chunk) // 4] = fine(two).astype(BF16)
        three = pooled(two, pool_c, lines1 // 2, across // 2)
        o3[:, start // 16:(start + chunk) // 16] = fine(three).astype(BF16)

    for line in lines:
        slot = line[2]

        @pl.when(inside(line[0], 0))
        def _(slot=slot):
            pltpu.make_async_copy(edge_rows.at[slot], edge_rows.at[slot], row_send.at[slot]).wait()

    for corner in corners:
        slot = corner[3]

        @pl.when(inside(corner[0], corner[1]))
        def _(slot=slot):
            pltpu.make_async_copy(edge_in.at[slot], edge_in.at[slot], edge_send.at[slot]).wait()

    for phase, slots in enumerate((stat_one, stat_two)):
        gone = slots.at[pl.ds(0, devices - 1)]
        pltpu.make_async_copy(gone, gone, all_send.at[phase]).wait()
    pltpu.make_async_copy(others, others, all_send.at[2]).wait()


def body(row_tiles, col_tiles, frame_one, frame_two, first_kernel, second_kernel, out_proj, out_bias):
    rows, cols, cin = frame_one.shape
    channels = out_proj.shape[1]
    devices = row_tiles * col_tiles
    queries = rows * cols
    keys = devices * queries // 4
    wide = cols + 16
    chunk = min(keys, 2048)
    vmem = pltpu.VMEM
    anywhere = pl.BlockSpec(memory_space=pl.ANY)
    local = pl.BlockSpec(memory_space=pltpu.VMEM)
    outs = pl.pallas_call(
        functools.partial(kernel, row_tiles, col_tiles, rows, cols),
        out_shape=[
            jax.ShapeDtypeStruct((queries, keys), BF16),
            jax.ShapeDtypeStruct((queries, keys // 4), BF16),
            jax.ShapeDtypeStruct((queries, keys // 16), BF16),
        ],
        in_specs=[anywhere] * 6,
        out_specs=[local] * 3,
        scratch_shapes=[
            vmem((3, 3 * cin, cin), BF16),
            vmem((3, 3 * cin, cin), BF16),
            vmem((cin, channels), BF16),
            vmem((1, channels), F32),
            vmem((2, rows, cols, cin), BF16),
            vmem((4, 2, cols, cin), BF16),
            vmem((2, 8, cin), F32),
            vmem((6, 8, cin), F32),
            vmem((2, 6, cols + 32, cin), F32),
            vmem((2, 6, wide, 3 * cin), BF16),
            vmem((2, 2, wide, cin), F32),
            vmem((2, 2, wide, cin), F32),
            vmem((2, 4, cols + 32, cin), F32),
            vmem((2, 4, cols, 3 * cin), BF16),
            vmem((devices, 4, cin), F32),
            vmem((devices, 4, cin), F32),
            vmem((keys, cin), BF16),
            vmem((cols, cin), F32),
            vmem((chunk // 2, cin), F32),
            vmem((chunk // 8, cin), F32),
            pltpu.SemaphoreType.DMA((6,)),
            pltpu.SemaphoreType.DMA((4,)),
            pltpu.SemaphoreType.DMA((4,)),
            pltpu.SemaphoreType.DMA((6,)),
            pltpu.SemaphoreType.DMA((6,)),
            pltpu.SemaphoreType.DMA((3,)),
            pltpu.SemaphoreType.DMA((3,)),
        ],
        compiler_params=pltpu.CompilerParams(
            collective_id=0, has_side_effects=True, vmem_limit_bytes=48 * 1024 * 1024
        ),
    )(
        frame_one, frame_two,
        first_kernel.reshape(3, 3 * cin, cin), second_kernel.reshape(3, 3 * cin, cin),
        out_proj, out_bias.reshape(1, channels),
    )
    return tuple(out.reshape(rows, cols, -1) for out in outs)


def solution(mesh):
    in_specs = (P("tr", "tc", None), P("tr", "tc", None), P(), P(), P(), P())
    out_specs = (P("tr", "tc", None), P("tr", "tc", None), P("tr", "tc", None))
    step = functools.partial(body, mesh.shape["tr"], mesh.shape["tc"])
    return jax.shard_map(step, mesh=mesh, in_specs=in_specs, out_specs=out_specs, check_vma=False)
```

```python
import functools
import math

import jax
import jax.numpy as jnp
from jax import lax
from jax.experimental import pallas as pl
from jax.experimental.pallas import tpu as pltpu
from jax.sharding import PartitionSpec as P

MESH = pl.DeviceIdType.MESH
F32 = jnp.float32
BF16 = jnp.bfloat16


def dot_t(a, b):
    return lax.dot_general(a, b, (((1,), (1,)), ((), ())), preferred_element_type=F32)


def split(values):
    high = values.astype(BF16)
    low = (values - high.astype(F32)).astype(BF16)
    return high, low


def kernel(
    row_tiles, col_tiles, rows, cols,
    f1, f2, w1_hbm, w2_hbm, wp_hbm, bias_hbm,
    keys, query_out, offset_out,
    w1, w2, wp, bias,
    tiles, edge_rows, edge_out, edge_in,
    grid, patches, conv_own, conv_edge, hidden, patches2,
    near_one, far_one, near_two, far_two, pool_a,
    in_sem, row_send, row_recv, edge_send, edge_recv, all_send, all_recv, line_recv,
):
    tr = lax.axis_index("tr")
    tc = lax.axis_index("tc")
    devices = row_tiles * col_tiles
    me = tr * col_tiles + tc
    positions = float(devices * rows * cols)
    channels = wp.shape[1]
    pooled_cols = cols // 2

    loads = [
        pltpu.make_async_copy(f1, tiles.at[0], in_sem.at[0]),
        pltpu.make_async_copy(f2, tiles.at[1], in_sem.at[1]),
        pltpu.make_async_copy(w1_hbm, w1, in_sem.at[2]),
        pltpu.make_async_copy(w2_hbm, w2, in_sem.at[3]),
        pltpu.make_async_copy(wp_hbm, wp, in_sem.at[4]),
        pltpu.make_async_copy(bias_hbm, bias, in_sem.at[5]),
    ]
    for load in loads:
        load.start()

    edge_rows[...] = jnp.zeros_like(edge_rows)
    edge_in[...] = jnp.zeros_like(edge_in)

    def inside(down, side):
        row = tr + down
        col = tc + side
        return (row >= 0) & (row < row_tiles) & (col >= 0) & (col < col_tiles)

    def along_rows(step):
        return (lax.rem(tr + step, row_tiles), tc)

    def along_cols(step):
        return (tr, lax.rem(tc + step, col_tiles))

    def each(count, act):
        if count <= 8:
            for step in sorted(range(1, count), key=lambda s: min(s, count - s)):
                act(step)
        else:
            def turn(step, carried):
                act(step)
                return carried

            lax.fori_loop(1, count, turn, 0)

    barrier = pltpu.get_barrier_semaphore()

    def greet(place):
        pl.semaphore_signal(barrier, inc=1, device_id=place, device_id_type=MESH)

    each(row_tiles, lambda step: greet(along_rows(step)))
    each(col_tiles, lambda step: greet(along_cols(step)))
    greeted = row_tiles + col_tiles - 2
    for down, side in ((1, 1), (1, -1), (-1, 1), (-1, -1)):
        @pl.when(inside(down, side))
        def _(down=down, side=side):
            greet((tr + down, tc + side))

        greeted = greeted + inside(down, side).astype(jnp.int32)

    loads[0].wait()
    loads[1].wait()
    left = 16
    right = left + cols
    for f in range(2):
        for y in range(2):
            values = tiles[f, y].astype(F32)
            grid[f, 2 + y, left:right, :] = values
            line = f * 4 + y * 2
            edge_out[0, line:line + 2, :] = values[0:2]
            edge_out[1, line:line + 2, :] = values[cols - 2:cols]

    pl.semaphore_wait(barrier, greeted)

    corners = [
        (0, 1, 1, 0), (0, -1, 0, 1),
        (1, 1, 1, 2), (1, -1, 0, 3),
        (-1, 1, 1, 4), (-1, -1, 0, 5),
    ]
    lines = [(1, 1, 0), (-1, 0, 1), (1, 0, 2), (-1, 1, 3)]

    def row_copies(down, row, slot):
        return [
            pltpu.make_async_remote_copy(
                src_ref=frame.at[row], dst_ref=edge_rows.at[slot, f],
                send_sem=row_send.at[slot], recv_sem=row_recv.at[slot],
                device_id=(tr + down, tc), device_id_type=MESH,
            )
            for f, frame in enumerate((f1, f2))
        ]

    def edge_copy(down, side, which, slot):
        return pltpu.make_async_remote_copy(
            src_ref=edge_out.at[which], dst_ref=edge_in.at[slot],
            send_sem=edge_send.at[slot], recv_sem=edge_recv.at[slot],
            device_id=(tr + down, tc + side), device_id_type=MESH,
        )

    def send_row(line):
        @pl.when(inside(line[0], 0))
        def _():
            for copy in row_copies(*line):
                copy.start()

    def send_edge(corner):
        @pl.when(inside(corner[0], corner[1]))
        def _():
            edge_copy(*corner).start()

    def await_row(line):
        slot = line[2]

        @pl.when(inside(-line[0], 0))
        def _():
            pltpu.make_async_copy(edge_rows.at[slot], edge_rows.at[slot], row_recv.at[slot]).wait()

    def await_edge(corner):
        slot = corner[3]

        @pl.when(inside(-corner[0], -corner[1]))
        def _():
            pltpu.make_async_copy(edge_in.at[slot], edge_in.at[slot], edge_recv.at[slot]).wait()

    for line in lines[:2]:
        send_row(line)
    for corner in corners:
        send_edge(corner)
    for line in lines[2:]:
        send_row(line)

    def fill_row(y, slot):
        for f in range(2):
            grid[f, y, left:right, :] = edge_rows[slot, f].astype(F32)

    def fill_edges(y, slot, base):
        for f in range(2):
            line = f * 4 + base * 2
            grid[f, y, left - 2:left, :] = edge_in[slot, line:line + 2, :]
            grid[f, y, right:right + 2, :] = edge_in[slot + 1, line:line + 2, :]

    wide = cols + 16

    def fill_patches(y):
        for f in range(2):
            for j in range(3):
                start = left - 9 + j
                patches[f, y, :, j * 128:(j + 1) * 128] = grid[f, y, start:start + wide, :].astype(BF16)

    for line in lines[:2]:
        await_row(line)
    for corner in corners:
        await_edge(corner)
    fill_row(1, 0)
    fill_row(4, 1)
    for y in range(2):
        fill_edges(2 + y, 0, y)
        fill_edges(0 + y, 2, y)
        fill_edges(4 + y, 4, y)
    for y in range(1, 5):
        fill_patches(y)

    loads[2].wait()

    def convolve(first_row, count):
        total = None
        for i in range(3):
            window = patches[:, first_row - 1 + i:first_row - 1 + i + count]
            part = jnp.dot(window.reshape(2 * count * wide, 384), w1[i], preferred_element_type=F32)
            total = part if total is None else total + part
        return total.reshape(2, count, wide, 128)

    def give(slots, mine, place, phase):
        pltpu.make_async_remote_copy(
            src_ref=slots.at[mine], dst_ref=slots.at[mine],
            send_sem=all_send.at[phase], recv_sem=all_recv.at[phase],
            device_id=place, device_id_type=MESH,
        ).start()

    def arrived(slots, count, sem):
        others = slots.at[pl.ds(0, count)]
        pltpu.make_async_copy(others, others, sem).wait()

    def share(stats, slots, phase):
        slots[tc] = stats
        each(col_tiles, lambda step: give(slots, tc, along_cols(step), phase))

    def pass_on(near, far, phase):
        arrived(near, col_tiles - 1, all_recv.at[phase])
        far[tr] = jnp.sum(near[...], axis=0)
        each(row_tiles, lambda step: give(far, tr, along_rows(step), phase + 1))

    def sums_of(values):
        total = jnp.sum(values, axis=(1, 2))
        squares = jnp.sum(values * values, axis=(1, 2))
        return jnp.concatenate([total, squares], axis=0)

    def collect(far, phase):
        arrived(far, row_tiles - 1, all_recv.at[phase])
        total = jnp.sum(far[...], axis=0) / positions
        centre = total[0:2]
        spread = total[2:4] - centre * centre
        return centre[:, None, None, :], lax.rsqrt(spread + 1e-05)[:, None, None, :]

    own = convolve(2, 2)
    conv_own[...] = own
    share(sums_of(own[:, :, 8:8 + cols]), near_one, 0)

    for line in lines[2:]:
        await_row(line)
    fill_row(0, 2)
    fill_row(5, 3)
    fill_patches(0)
    fill_patches(5)
    pass_on(near_one, far_one, 0)
    conv_edge[:, 0:1] = convolve(1, 1)
    conv_edge[:, 1:2] = convolve(4, 1)
    loads[3].wait()

    centre, inverse = collect(far_one, 1)
    spot = lax.broadcasted_iota(jnp.int32, (1, 1, wide, 128), 2)
    col_ok = ((spot >= 8) | (tc > 0)) & ((spot < 8 + cols) | (tc < col_tiles - 1))

    def normal(values, keep):
        return jnp.where(keep, jax.nn.relu((values - centre) * inverse), 0.0)

    hidden[:, 1:3, 8:8 + wide, :] = normal(conv_own[...], col_ok)
    hidden[:, 0:1, 8:8 + wide, :] = normal(conv_edge[:, 0:1], col_ok & (tr > 0))
    hidden[:, 3:4, 8:8 + wide, :] = normal(conv_edge[:, 1:2], col_ok & (tr < row_tiles - 1))
    for f in range(2):
        for y in range(4):
            for j in range(3):
                start = left - 1 + j
                patches2[f, y, :, j * 128:(j + 1) * 128] = hidden[f, y, start:start + cols, :].astype(BF16)
    second = None
    for i in range(3):
        window = patches2[:, i:i + 2].reshape(4 * cols, 384)
        part = jnp.dot(window, w2[i], preferred_element_type=F32)
        second = part if second is None else second + part
    second = second.reshape(2, 2, cols, 128)
    share(sums_of(second), near_two, 2)
    loads[4].wait()
    loads[5].wait()
    pass_on(near_two, far_two, 2)
    centre, inverse = collect(far_two, 3)
    blocks = jax.nn.relu(tiles[...].astype(F32) + jax.nn.relu((second - centre) * inverse)).astype(BF16)

    pool_a[0:cols, :] = blocks[1, 0].astype(F32) + blocks[1, 1].astype(F32)
    small = (pool_a[pl.ds(0, pooled_cols, stride=2), :] + pool_a[pl.ds(1, pooled_cols, stride=2), :]) * 0.25
    keys[tr, tc] = small.astype(BF16)

    def key_copy(row, place, send_sem, recv_sem):
        return pltpu.make_async_remote_copy(
            src_ref=keys.at[row, tc], dst_ref=keys.at[row, tc],
            send_sem=send_sem, recv_sem=recv_sem,
            device_id=place, device_id_type=MESH,
        )

    def spread_line(row):
        each(col_tiles, lambda step: key_copy(
            row, along_cols(step), all_send.at[5], all_recv.at[4]).start())

    each(row_tiles, lambda step: key_copy(
        tr, along_rows(step), all_send.at[4], line_recv.at[tr]).start())
    spread_line(tr)

    scale = 1.0 / math.sqrt(channels)
    feature = jnp.dot(blocks[0].reshape(2 * cols, 128), wp[...], preferred_element_type=F32) + bias[...]
    feature = feature.astype(BF16)
    offset = jnp.sum(feature.astype(F32) * bias[...], axis=1, keepdims=True) * scale
    high, low = split(dot_t(feature, wp[...]) * scale)
    queries = jnp.concatenate([high, low], axis=1)

    query_out[...] = queries
    offset_out[...] = jnp.broadcast_to(offset, offset_out.shape)

    def forward(step):
        row = lax.rem(tr + row_tiles - step, row_tiles)
        block = keys.at[row, tc]
        pltpu.make_async_copy(block, block, line_recv.at[row]).wait()
        spread_line(row)

    each(row_tiles, forward)
    cross = keys.at[:, pl.ds(0, col_tiles - 1)]
    pltpu.make_async_copy(cross, cross, all_recv.at[4]).wait()

    for line in lines:
        slot = line[2]

        @pl.when(inside(line[0], 0))
        def _(slot=slot):
            pltpu.make_async_copy(edge_rows.at[slot], edge_rows.at[slot], row_send.at[slot]).wait()

    for corner in corners:
        slot = corner[3]

        @pl.when(inside(corner[0], corner[1]))
        def _(slot=slot):
            pltpu.make_async_copy(edge_in.at[slot], edge_in.at[slot], edge_send.at[slot]).wait()

    arrived(near_one, col_tiles - 1, all_send.at[0])
    arrived(far_one, row_tiles - 1, all_send.at[1])
    arrived(near_two, col_tiles - 1, all_send.at[2])
    arrived(far_two, row_tiles - 1, all_send.at[3])
    line = keys.at[pl.ds(0, row_tiles - 1), 0]
    pltpu.make_async_copy(line, line, all_send.at[4]).wait()
    pltpu.make_async_copy(cross, cross, all_send.at[5]).wait()


def correlate(across, keys, query, offset_ref, o1, o2, o3, pool_b, pool_c):
    total_keys = keys.shape[0]
    chunk = min(total_keys, 2048)
    lines1 = chunk // across
    queries = query[...]
    high = queries[:, 0:128]
    offset = offset_ref[:, 0:1]

    def pooled(values, scratch, lines_in, width):
        pairs = jnp.sum(values.reshape(lines_in // 2, 2, width, 128), axis=1)
        count = lines_in // 2 * width
        scratch[0:count, :] = pairs.reshape(count, 128)
        half = count // 2
        return (scratch[pl.ds(0, half, stride=2), :] + scratch[pl.ds(1, half, stride=2), :]) * 0.25

    def fine(values):
        k_high, k_low = split(values)
        return dot_t(queries, jnp.concatenate([k_high, k_high], axis=1)) + dot_t(high, k_low) + offset

    for start in range(0, total_keys, chunk):
        part = keys[start:start + chunk, :]
        level = dot_t(queries, jnp.concatenate([part, part], axis=1)) + offset
        o1[:, start:start + chunk] = level.astype(BF16)
        two = pooled(part.astype(F32), pool_b, lines1, across)
        o2[:, start // 4:(start + chunk) // 4] = fine(two).astype(BF16)
        three = pooled(two, pool_c, lines1 // 2, across // 2)
        o3[:, start // 16:(start + chunk) // 16] = fine(three).astype(BF16)


def body(row_tiles, col_tiles, frame_one, frame_two, first_kernel, second_kernel, out_proj, out_bias):
    rows, cols, cin = frame_one.shape
    channels = out_proj.shape[1]
    devices = row_tiles * col_tiles
    queries = rows * cols
    keys = devices * queries // 4
    wide = cols + 16
    chunk = min(keys, 2048)
    vmem = pltpu.VMEM
    anywhere = pl.BlockSpec(memory_space=pl.ANY)
    local = pl.BlockSpec(memory_space=pltpu.VMEM)
    key_blocks, query, offset = pl.pallas_call(
        functools.partial(kernel, row_tiles, col_tiles, rows, cols),
        out_shape=[
            jax.ShapeDtypeStruct((row_tiles, col_tiles, cols // 2, cin), BF16),
            jax.ShapeDtypeStruct((queries, 2 * cin), BF16),
            jax.ShapeDtypeStruct((queries, 128), F32),
        ],
        in_specs=[anywhere] * 6,
        out_specs=[local] * 3,
        scratch_shapes=[
            vmem((3, 3 * cin, cin), BF16),
            vmem((3, 3 * cin, cin), BF16),
            vmem((cin, channels), BF16),
            vmem((1, channels), F32),
            vmem((2, rows, cols, cin), BF16),
            vmem((4, 2, cols, cin), BF16),
            vmem((2, 8, cin), F32),
            vmem((6, 8, cin), F32),
            vmem((2, 6, cols + 32, cin), F32),
            vmem((2, 6, wide, 3 * cin), BF16),
            vmem((2, 2, wide, cin), F32),
            vmem((2, 2, wide, cin), F32),
            vmem((2, 4, cols + 32, cin), F32),
            vmem((2, 4, cols, 3 * cin), BF16),
            vmem((col_tiles, 4, cin), F32),
            vmem((row_tiles, 4, cin), F32),
            vmem((col_tiles, 4, cin), F32),
            vmem((row_tiles, 4, cin), F32),
            vmem((cols, cin), F32),
            pltpu.SemaphoreType.DMA((6,)),
            pltpu.SemaphoreType.DMA((4,)),
            pltpu.SemaphoreType.DMA((4,)),
            pltpu.SemaphoreType.DMA((6,)),
            pltpu.SemaphoreType.DMA((6,)),
            pltpu.SemaphoreType.DMA((6,)),
            pltpu.SemaphoreType.DMA((5,)),
            pltpu.SemaphoreType.DMA((row_tiles,)),
        ],
        compiler_params=pltpu.CompilerParams(
            collective_id=0, has_side_effects=True, vmem_limit_bytes=48 * 1024 * 1024
        ),
    )(*[
        pltpu.with_memory_space_constraint(value, pltpu.HBM)
        for value in (
            frame_one, frame_two,
            first_kernel.reshape(3, 3 * cin, cin), second_kernel.reshape(3, 3 * cin, cin),
            out_proj, out_bias.reshape(1, channels),
        )
    ])
    outs = pl.pallas_call(
        functools.partial(correlate, col_tiles * cols // 2),
        out_shape=[
            jax.ShapeDtypeStruct((queries, keys), BF16),
            jax.ShapeDtypeStruct((queries, keys // 4), BF16),
            jax.ShapeDtypeStruct((queries, keys // 16), BF16),
        ],
        in_specs=[local] * 3,
        out_specs=[local] * 3,
        scratch_shapes=[vmem((chunk // 2, cin), F32), vmem((chunk // 8, cin), F32)],
        compiler_params=pltpu.CompilerParams(vmem_limit_bytes=24 * 1024 * 1024),
    )(key_blocks.reshape(keys, cin), query, offset)
    return tuple(out.reshape(rows, cols, -1) for out in outs)


def solution(mesh):
    in_specs = (P("tr", "tc", None), P("tr", "tc", None), P(), P(), P(), P())
    out_specs = (P("tr", "tc", None), P("tr", "tc", None), P("tr", "tc", None))
    step = functools.partial(body, mesh.shape["tr"], mesh.shape["tc"])
    return jax.shard_map(step, mesh=mesh, in_specs=in_specs, out_specs=out_specs, check_vma=False)
```

```python
import functools
import math

import jax
import jax.numpy as jnp
from jax import lax
from jax.experimental import pallas as pl
from jax.experimental.pallas import tpu as pltpu
from jax.sharding import PartitionSpec as P

MESH = pl.DeviceIdType.MESH
F32 = jnp.float32
BF16 = jnp.bfloat16


def dot_t(a, b):
    return lax.dot_general(a, b, (((1,), (1,)), ((), ())), preferred_element_type=F32)


def split(values):
    high = values.astype(BF16)
    low = (values - high.astype(F32)).astype(BF16)
    return high, low


def kernel(
    row_tiles, col_tiles, rows, cols,
    f1, f2, w1_hbm, w2_hbm, wp_hbm, bias_hbm,
    keys, query_out, offset_out,
    w1, w2, wp, bias,
    tiles, edge_rows, edge_out, edge_in,
    grid, patches, conv_own, conv_edge, hidden, patches2,
    stat_one, stat_two, pool_a,
    in_sem, row_send, row_recv, edge_send, edge_recv, all_send, all_recv,
):
    tr = lax.axis_index("tr")
    tc = lax.axis_index("tc")
    devices = row_tiles * col_tiles
    me = tr * col_tiles + tc
    positions = float(devices * rows * cols)
    channels = wp.shape[1]
    pooled_cols = cols // 2

    loads = [
        pltpu.make_async_copy(f1, tiles.at[0], in_sem.at[0]),
        pltpu.make_async_copy(f2, tiles.at[1], in_sem.at[1]),
        pltpu.make_async_copy(w1_hbm, w1, in_sem.at[2]),
        pltpu.make_async_copy(w2_hbm, w2, in_sem.at[3]),
        pltpu.make_async_copy(wp_hbm, wp, in_sem.at[4]),
        pltpu.make_async_copy(bias_hbm, bias, in_sem.at[5]),
    ]
    for load in loads:
        load.start()

    edge_rows[...] = jnp.zeros_like(edge_rows)
    edge_in[...] = jnp.zeros_like(edge_in)

    def inside(down, side):
        row = tr + down
        col = tc + side
        return (row >= 0) & (row < row_tiles) & (col >= 0) & (col < col_tiles)

    def each(act):
        def turn(step, carried=0):
            other = lax.rem(me + step, devices)
            act((other // col_tiles, lax.rem(other, col_tiles)))
            return carried

        if devices <= 32:
            for step in sorted(range(1, devices), key=lambda s: -min(s, devices - s)):
                turn(step)
        else:
            lax.fori_loop(1, devices, turn, 0)

    barrier = pltpu.get_barrier_semaphore()

    def greet(place):
        pl.semaphore_signal(barrier, inc=1, device_id=place, device_id_type=MESH)

    each(greet)

    loads[0].wait()
    loads[1].wait()
    left = 16
    right = left + cols
    for f in range(2):
        for y in range(2):
            values = tiles[f, y].astype(F32)
            grid[f, 2 + y, left:right, :] = values
            line = f * 4 + y * 2
            edge_out[0, line:line + 2, :] = values[0:2]
            edge_out[1, line:line + 2, :] = values[cols - 2:cols]

    pl.semaphore_wait(barrier, devices - 1)

    corners = [
        (0, 1, 1, 0), (0, -1, 0, 1),
        (1, 1, 1, 2), (1, -1, 0, 3),
        (-1, 1, 1, 4), (-1, -1, 0, 5),
    ]
    lines = [(1, 1, 0), (-1, 0, 1), (1, 0, 2), (-1, 1, 3)]

    def row_copy(down, row, slot):
        return pltpu.make_async_remote_copy(
            src_ref=tiles.at[:, row], dst_ref=edge_rows.at[slot],
            send_sem=row_send.at[slot], recv_sem=row_recv.at[slot],
            device_id=(tr + down, tc), device_id_type=MESH,
        )

    def edge_copy(down, side, which, slot):
        return pltpu.make_async_remote_copy(
            src_ref=edge_out.at[which], dst_ref=edge_in.at[slot],
            send_sem=edge_send.at[slot], recv_sem=edge_recv.at[slot],
            device_id=(tr + down, tc + side), device_id_type=MESH,
        )

    def send_row(line):
        @pl.when(inside(line[0], 0))
        def _():
            row_copy(*line).start()

    def send_edge(corner):
        @pl.when(inside(corner[0], corner[1]))
        def _():
            edge_copy(*corner).start()

    def await_row(line):
        slot = line[2]

        @pl.when(inside(-line[0], 0))
        def _():
            pltpu.make_async_copy(edge_rows.at[slot], edge_rows.at[slot], row_recv.at[slot]).wait()

    def await_edge(corner):
        slot = corner[3]

        @pl.when(inside(-corner[0], -corner[1]))
        def _():
            pltpu.make_async_copy(edge_in.at[slot], edge_in.at[slot], edge_recv.at[slot]).wait()

    for corner in corners:
        send_edge(corner)
    for line in lines:
        send_row(line)

    def fill_row(y, slot):
        for f in range(2):
            grid[f, y, left:right, :] = edge_rows[slot, f].astype(F32)

    def fill_edges(y, slot, base):
        for f in range(2):
            line = f * 4 + base * 2
            grid[f, y, left - 2:left, :] = edge_in[slot, line:line + 2, :]
            grid[f, y, right:right + 2, :] = edge_in[slot + 1, line:line + 2, :]

    wide = cols + 16

    def fill_patches(y):
        for f in range(2):
            for j in range(3):
                start = left - 9 + j
                patches[f, y, :, j * 128:(j + 1) * 128] = grid[f, y, start:start + wide, :].astype(BF16)

    def patch(first, *others):
        parts = [patches[:, y].reshape(2 * wide, 384) for y in (first, *others)]
        return parts[0] if len(parts) == 1 else jnp.concatenate(parts, axis=1)

    def times(window, weights):
        return jnp.dot(window, weights, preferred_element_type=F32)

    def middle(weights):
        return jnp.concatenate([weights[384:1152], weights[0:768]], axis=1)

    for corner in corners[:2]:
        await_edge(corner)
    for y in range(2):
        fill_edges(2 + y, 0, y)
        fill_patches(2 + y)
    loads[2].wait()
    both = times(patch(2, 3), middle(w1))
    for line in lines[:2]:
        await_row(line)
    for corner in corners[2:]:
        await_edge(corner)
    fill_row(1, 0)
    fill_row(4, 1)
    for y in range(2):
        fill_edges(0 + y, 2, y)
        fill_edges(4 + y, 4, y)
    fill_patches(1)
    fill_patches(4)
    upper = both[:, 0:128] + times(patch(1), w1[0:384])
    lower = both[:, 128:256] + times(patch(4), w1[768:1152])
    conv_own[:, 0] = upper.reshape(2, wide, 128)
    conv_own[:, 1] = lower.reshape(2, wide, 128)

    def share(stats, slots, phase):
        slots[me] = stats
        each(lambda place: pltpu.make_async_remote_copy(
            src_ref=slots.at[me], dst_ref=slots.at[me],
            send_sem=all_send.at[phase], recv_sem=all_recv.at[phase],
            device_id=place, device_id_type=MESH,
        ).start())

    def arrived(slots, sem):
        others = slots.at[pl.ds(0, devices - 1)]
        pltpu.make_async_copy(others, others, sem).wait()

    def sums_of(values):
        total = jnp.sum(values, axis=(1, 2))
        squares = jnp.sum(values * values, axis=(1, 2))
        return jnp.concatenate([total, squares], axis=0)

    def collect(slots, phase):
        arrived(slots, all_recv.at[phase])
        total = jnp.sum(slots[...], axis=0) / positions
        centre = total[0:2]
        spread = total[2:4] - centre * centre
        return centre[:, None, None, :], lax.rsqrt(spread + 1e-05)[:, None, None, :]

    share(sums_of(conv_own[:, :, 8:8 + cols]), stat_one, 0)

    for line in lines[2:]:
        await_row(line)
    fill_row(0, 2)
    fill_row(5, 3)
    fill_patches(0)
    fill_patches(5)
    conv_edge[:, 0] = times(patch(0, 1, 2), w1[...]).reshape(2, wide, 128)
    conv_edge[:, 1] = times(patch(3, 4, 5), w1[...]).reshape(2, wide, 128)
    loads[3].wait()

    centre, inverse = collect(stat_one, 0)
    spot = lax.broadcasted_iota(jnp.int32, (1, 1, wide, 128), 2)
    col_ok = ((spot >= 8) | (tc > 0)) & ((spot < 8 + cols) | (tc < col_tiles - 1))

    def normal(values, keep):
        return jnp.where(keep, jax.nn.relu((values - centre) * inverse), 0.0)

    hidden[:, 1:3, 8:8 + wide, :] = normal(conv_own[...], col_ok)
    hidden[:, 0:1, 8:8 + wide, :] = normal(conv_edge[:, 0:1], col_ok & (tr > 0))
    hidden[:, 3:4, 8:8 + wide, :] = normal(conv_edge[:, 1:2], col_ok & (tr < row_tiles - 1))
    for f in range(2):
        for y in range(4):
            for j in range(3):
                start = left - 1 + j
                patches2[f, y, :, j * 128:(j + 1) * 128] = hidden[f, y, start:start + cols, :].astype(BF16)
    lines2 = [patches2[:, y].reshape(2 * cols, 384) for y in range(4)]
    both = times(jnp.concatenate(lines2[1:3], axis=1), middle(w2))
    upper = both[:, 0:128] + times(lines2[0], w2[0:384])
    lower = both[:, 128:256] + times(lines2[3], w2[768:1152])
    second = jnp.stack([upper.reshape(2, cols, 128), lower.reshape(2, cols, 128)], axis=1)
    share(sums_of(second), stat_two, 1)
    loads[4].wait()
    loads[5].wait()
    centre, inverse = collect(stat_two, 1)
    blocks = jax.nn.relu(tiles[...].astype(F32) + jax.nn.relu((second - centre) * inverse)).astype(BF16)

    pool_a[0:cols, :] = blocks[1, 0].astype(F32) + blocks[1, 1].astype(F32)
    small = (pool_a[pl.ds(0, pooled_cols, stride=2), :] + pool_a[pl.ds(1, pooled_cols, stride=2), :]) * 0.25
    keys[me] = small.astype(BF16)
    each(lambda place: pltpu.make_async_remote_copy(
        src_ref=keys.at[me], dst_ref=keys.at[me],
        send_sem=all_send.at[2], recv_sem=all_recv.at[2],
        device_id=place, device_id_type=MESH,
    ).start())

    scale = 1.0 / math.sqrt(channels)
    feature = jnp.dot(blocks[0].reshape(2 * cols, 128), wp[...], preferred_element_type=F32) + bias[...]
    feature = feature.astype(BF16)
    offset = jnp.sum(feature.astype(F32) * bias[...], axis=1, keepdims=True) * scale
    high, low = split(dot_t(feature, wp[...]) * scale)
    queries = jnp.concatenate([high, low], axis=1)

    query_out[...] = queries
    offset_out[...] = jnp.broadcast_to(offset, offset_out.shape)

    arrived(keys, all_recv.at[2])

    for line in lines:
        slot = line[2]

        @pl.when(inside(line[0], 0))
        def _(slot=slot):
            pltpu.make_async_copy(edge_rows.at[slot], edge_rows.at[slot], row_send.at[slot]).wait()

    for corner in corners:
        slot = corner[3]

        @pl.when(inside(corner[0], corner[1]))
        def _(slot=slot):
            pltpu.make_async_copy(edge_in.at[slot], edge_in.at[slot], edge_send.at[slot]).wait()

    for phase, slots in enumerate((stat_one, stat_two, keys)):
        arrived(slots, all_send.at[phase])


def correlate(across, keys, query, offset_ref, o1, o2, o3, pool_b, pool_c):
    total_keys = keys.shape[0]
    chunk = min(total_keys, 2048)
    lines1 = chunk // across
    queries = query[...]
    high = queries[:, 0:128]
    offset = offset_ref[:, 0:1]

    def pooled(values, scratch, lines_in, width):
        pairs = jnp.sum(values.reshape(lines_in // 2, 2, width, 128), axis=1)
        count = lines_in // 2 * width
        scratch[0:count, :] = pairs.reshape(count, 128)
        half = count // 2
        return (scratch[pl.ds(0, half, stride=2), :] + scratch[pl.ds(1, half, stride=2), :]) * 0.25

    def fine(values):
        k_high, k_low = split(values)
        return dot_t(queries, jnp.concatenate([k_high, k_high], axis=1)) + dot_t(high, k_low) + offset

    for start in range(0, total_keys, chunk):
        part = keys[start:start + chunk, :]
        level = dot_t(queries, jnp.concatenate([part, part], axis=1)) + offset
        o1[:, start:start + chunk] = level.astype(BF16)
        two = pooled(part.astype(F32), pool_b, lines1, across)
        o2[:, start // 4:(start + chunk) // 4] = fine(two).astype(BF16)
        three = pooled(two, pool_c, lines1 // 2, across // 2)
        o3[:, start // 16:(start + chunk) // 16] = fine(three).astype(BF16)


def body(row_tiles, col_tiles, frame_one, frame_two, first_kernel, second_kernel, out_proj, out_bias):
    rows, cols, cin = frame_one.shape
    channels = out_proj.shape[1]
    devices = row_tiles * col_tiles
    queries = rows * cols
    keys = devices * queries // 4
    wide = cols + 16
    chunk = min(keys, 2048)
    vmem = pltpu.VMEM
    anywhere = pl.BlockSpec(memory_space=pl.ANY)
    local = pl.BlockSpec(memory_space=pltpu.VMEM)
    key_blocks, query, offset = pl.pallas_call(
        functools.partial(kernel, row_tiles, col_tiles, rows, cols),
        out_shape=[
            jax.ShapeDtypeStruct((devices, cols // 2, cin), BF16),
            jax.ShapeDtypeStruct((queries, 2 * cin), BF16),
            jax.ShapeDtypeStruct((queries, 128), F32),
        ],
        in_specs=[anywhere] * 6,
        out_specs=[local] * 3,
        scratch_shapes=[
            vmem((9 * cin, cin), BF16),
            vmem((9 * cin, cin), BF16),
            vmem((cin, channels), BF16),
            vmem((1, channels), F32),
            vmem((2, rows, cols, cin), BF16),
            vmem((4, 2, cols, cin), BF16),
            vmem((2, 8, cin), F32),
            vmem((6, 8, cin), F32),
            vmem((2, 6, cols + 32, cin), F32),
            vmem((2, 6, wide, 3 * cin), BF16),
            vmem((2, 2, wide, cin), F32),
            vmem((2, 2, wide, cin), F32),
            vmem((2, 4, cols + 32, cin), F32),
            vmem((2, 4, cols, 3 * cin), BF16),
            vmem((devices, 4, cin), F32),
            vmem((devices, 4, cin), F32),
            vmem((cols, cin), F32),
            pltpu.SemaphoreType.DMA((6,)),
            pltpu.SemaphoreType.DMA((4,)),
            pltpu.SemaphoreType.DMA((4,)),
            pltpu.SemaphoreType.DMA((6,)),
            pltpu.SemaphoreType.DMA((6,)),
            pltpu.SemaphoreType.DMA((3,)),
            pltpu.SemaphoreType.DMA((3,)),
        ],
        compiler_params=pltpu.CompilerParams(
            collective_id=0, has_side_effects=True, vmem_limit_bytes=48 * 1024 * 1024
        ),
    )(*[
        pltpu.with_memory_space_constraint(value, pltpu.HBM)
        for value in (
            frame_one, frame_two,
            first_kernel.reshape(9 * cin, cin), second_kernel.reshape(9 * cin, cin),
            out_proj, out_bias.reshape(1, channels),
        )
    ])
    outs = pl.pallas_call(
        functools.partial(correlate, col_tiles * cols // 2),
        out_shape=[
            jax.ShapeDtypeStruct((queries, keys), BF16),
            jax.ShapeDtypeStruct((queries, keys // 4), BF16),
            jax.ShapeDtypeStruct((queries, keys // 16), BF16),
        ],
        in_specs=[local] * 3,
        out_specs=[local] * 3,
        scratch_shapes=[vmem((chunk // 2, cin), F32), vmem((chunk // 8, cin), F32)],
        compiler_params=pltpu.CompilerParams(vmem_limit_bytes=24 * 1024 * 1024),
    )(key_blocks.reshape(keys, cin), query, offset)
    return tuple(out.reshape(rows, cols, -1) for out in outs)


def solution(mesh):
    in_specs = (P("tr", "tc", None), P("tr", "tc", None), P(), P(), P(), P())
    out_specs = (P("tr", "tc", None), P("tr", "tc", None), P("tr", "tc", None))
    step = functools.partial(body, mesh.shape["tr"], mesh.shape["tc"])
    return jax.shard_map(step, mesh=mesh, in_specs=in_specs, out_specs=out_specs, check_vma=False)
```

```python
import functools
import math

import jax
import jax.numpy as jnp
from jax import lax
from jax.experimental import pallas as pl
from jax.experimental.pallas import tpu as pltpu
from jax.sharding import PartitionSpec as P

MESH = pl.DeviceIdType.MESH
FLAT = pl.DeviceIdType.LOGICAL
F32 = jnp.float32
BF16 = jnp.bfloat16


def dot_t(a, b):
    return lax.dot_general(a, b, (((1,), (1,)), ((), ())), preferred_element_type=F32)


def split(values):
    high = values.astype(BF16)
    low = (values - high.astype(F32)).astype(BF16)
    return high, low


def kernel(
    row_tiles, col_tiles, rows, cols,
    f1, f2, w1_hbm, w2_hbm, wp_hbm, bias_hbm,
    keys, query_out, offset_out,
    w1, w2, wp, bias,
    tiles, edge_rows, edge_out, edge_in,
    grid, patches, conv, hidden, patches2, conv2,
    stats, pool_a,
    in_sem, row_send, row_recv, edge_send, edge_recv, all_send, all_recv,
):
    tr = lax.axis_index("tr")
    tc = lax.axis_index("tc")
    devices = row_tiles * col_tiles
    me = tr * col_tiles + tc
    positions = float(devices * rows * cols)
    channels = wp.shape[1]
    pooled_cols = cols // 2

    loads = [
        pltpu.make_async_copy(f1, tiles.at[0], in_sem.at[0]),
        pltpu.make_async_copy(f2, tiles.at[1], in_sem.at[1]),
        pltpu.make_async_copy(w1_hbm, w1, in_sem.at[2]),
        pltpu.make_async_copy(w2_hbm, w2, in_sem.at[3]),
        pltpu.make_async_copy(wp_hbm, wp, in_sem.at[4]),
        pltpu.make_async_copy(bias_hbm, bias, in_sem.at[5]),
    ]
    for load in loads:
        load.start()

    edge_rows[...] = jnp.zeros_like(edge_rows)
    edge_in[...] = jnp.zeros_like(edge_in)

    def inside(down, side):
        row = tr + down
        col = tc + side
        return (row >= 0) & (row < row_tiles) & (col >= 0) & (col < col_tiles)

    far_first = sorted(range(1, devices), key=lambda s: -min(s, devices - s))
    close = (1, col_tiles - 1, col_tiles, col_tiles + 1)
    close_first = sorted(far_first, key=lambda s: min(s, devices - s) not in close)

    def each(act, order):
        def turn(step, carried=0):
            other = me + step
            act(jnp.where(other < devices, other, other - devices))
            return carried

        if devices <= 32:
            for step in order:
                turn(step)
        else:
            lax.fori_loop(1, devices, turn, 0)

    barrier = pltpu.get_barrier_semaphore()

    def greet(index):
        pl.semaphore_signal(barrier, inc=1, device_id=index, device_id_type=FLAT)

    each(greet, close_first)

    loads[0].wait()
    loads[1].wait()
    left = 16
    right = left + cols
    for f in range(2):
        for y in range(2):
            values = tiles[f, y].astype(F32)
            grid[f, 2 + y, left:right, :] = values
            line = f * 4 + y * 2
            edge_out[0, line:line + 2, :] = values[0:2]
            edge_out[1, line:line + 2, :] = values[cols - 2:cols]

    pl.semaphore_wait(barrier, devices - 1)

    corners = [
        (0, 1, 1, 0), (0, -1, 0, 1),
        (1, 1, 1, 2), (1, -1, 0, 3),
        (-1, 1, 1, 4), (-1, -1, 0, 5),
    ]
    lines = [(1, 1, 0), (-1, 0, 1), (1, 0, 2), (-1, 1, 3)]

    def row_copy(down, row, slot):
        return pltpu.make_async_remote_copy(
            src_ref=tiles.at[:, row], dst_ref=edge_rows.at[slot],
            send_sem=row_send.at[slot], recv_sem=row_recv.at[slot],
            device_id=(tr + down, tc), device_id_type=MESH,
        )

    def edge_copy(down, side, which, slot):
        return pltpu.make_async_remote_copy(
            src_ref=edge_out.at[which], dst_ref=edge_in.at[slot],
            send_sem=edge_send.at[slot], recv_sem=edge_recv.at[slot],
            device_id=(tr + down, tc + side), device_id_type=MESH,
        )

    def send_row(line):
        @pl.when(inside(line[0], 0))
        def _():
            row_copy(*line).start()

    def send_edge(corner):
        @pl.when(inside(corner[0], corner[1]))
        def _():
            edge_copy(*corner).start()

    def await_row(line):
        slot = line[2]

        @pl.when(inside(-line[0], 0))
        def _():
            pltpu.make_async_copy(edge_rows.at[slot], edge_rows.at[slot], row_recv.at[slot]).wait()

    def await_edge(corner):
        slot = corner[3]

        @pl.when(inside(-corner[0], -corner[1]))
        def _():
            pltpu.make_async_copy(edge_in.at[slot], edge_in.at[slot], edge_recv.at[slot]).wait()

    for corner in corners:
        send_edge(corner)
    for line in lines:
        send_row(line)

    wide = cols + 16

    def fill_row(f, y, slot):
        grid[f, y, left:right, :] = edge_rows[slot, f].astype(F32)

    def fill_edges(f, y, slot, base):
        line = f * 4 + base * 2
        grid[f, y, left - 2:left, :] = edge_in[slot, line:line + 2, :]
        grid[f, y, right:right + 2, :] = edge_in[slot + 1, line:line + 2, :]

    def fill_patches(f, y):
        for j in range(3):
            start = left - 9 + j
            patches[f, y, :, j * 128:(j + 1) * 128] = grid[f, y, start:start + wide, :].astype(BF16)

    def patch(source, f, *lines_in):
        return jnp.concatenate([source[f, y] for y in lines_in], axis=1)

    def times(window, weights):
        return jnp.dot(window, weights, preferred_element_type=F32)

    def middle(weights):
        return jnp.concatenate([weights[384:1152], weights[0:768]], axis=1)

    def send_block(slots, phase):
        each(lambda index: pltpu.make_async_remote_copy(
            src_ref=slots.at[me], dst_ref=slots.at[me],
            send_sem=all_send.at[phase], recv_sem=all_recv.at[phase],
            device_id=index, device_id_type=FLAT,
        ).start(), far_first)

    def arrived(slots, sem):
        others = slots.at[pl.ds(0, devices - 1)]
        pltpu.make_async_copy(others, others, sem).wait()

    def share(upper, lower, phase):
        total = jnp.sum(upper + lower, axis=0, keepdims=True)
        squares = jnp.sum(upper * upper + lower * lower, axis=0, keepdims=True)
        stats[phase, me] = jnp.concatenate([total, squares], axis=0)
        send_block(stats.at[phase], phase)

    def collect(phase):
        arrived(stats.at[phase], all_recv.at[phase])
        total = jnp.sum(stats[phase], axis=0) / positions
        centre = total[0:1]
        spread = total[1:2] - centre * centre
        return centre, lax.rsqrt(spread + 1e-05)

    spot = lax.broadcasted_iota(jnp.int32, (wide, 128), 0)
    col_ok = ((spot >= 8) | (tc > 0)) & ((spot < 8 + cols) | (tc < col_tiles - 1))
    row_ok = (col_ok & (tr > 0), col_ok, col_ok, col_ok & (tr < row_tiles - 1))

    def start_own(f):
        for y in range(2):
            fill_edges(f, 2 + y, 0, y)
            fill_patches(f, 2 + y)
        return times(patch(patches, f, 2, 3), middle(w1))

    def finish_own(f, both):
        fill_row(f, 1, 0)
        fill_row(f, 4, 1)
        for y in range(2):
            fill_edges(f, 0 + y, 2, y)
            fill_edges(f, 4 + y, 4, y)
        fill_patches(f, 1)
        fill_patches(f, 4)
        conv[f, 1] = both[:, 0:128] + times(patches[f, 1], w1[0:384])
        conv[f, 2] = both[:, 128:256] + times(patches[f, 4], w1[768:1152])
        share(conv[f, 1, 8:8 + cols], conv[f, 2, 8:8 + cols], f)

    def edge_lines(f):
        fill_row(f, 0, 2)
        fill_row(f, 5, 3)
        fill_patches(f, 0)
        fill_patches(f, 5)
        conv[f, 0] = times(patch(patches, f, 0, 1, 2), w1[...])
        conv[f, 3] = times(patch(patches, f, 3, 4, 5), w1[...])

    def second_half(f):
        centre, inverse = collect(f)
        for y in range(4):
            values = jax.nn.relu((conv[f, y] - centre) * inverse)
            hidden[f, y, 8:8 + wide, :] = jnp.where(row_ok[y], values, 0.0)
            for j in range(3):
                start = left - 1 + j
                patches2[f, y, :, j * 128:(j + 1) * 128] = hidden[f, y, start:start + cols, :].astype(BF16)
        both = times(patch(patches2, f, 1, 2), middle(w2))
        upper = both[:, 0:128] + times(patches2[f, 0], w2[0:384])
        lower = both[:, 128:256] + times(patches2[f, 3], w2[768:1152])
        share(upper, lower, 2 + f)
        conv2[f, 0] = upper
        conv2[f, 1] = lower

    def blocks_of(f):
        centre, inverse = collect(2 + f)
        values = jax.nn.relu((conv2[f] - centre) * inverse)
        return jax.nn.relu(tiles[f].astype(F32) + values).astype(BF16)

    for corner in corners[:2]:
        await_edge(corner)
    loads[2].wait()
    both = start_own(1)
    for line in lines[:2]:
        await_row(line)
    for corner in corners[2:]:
        await_edge(corner)
    finish_own(1, both)
    finish_own(0, start_own(0))
    for line in lines[2:]:
        await_row(line)
    edge_lines(1)
    loads[3].wait()
    second_half(1)
    edge_lines(0)
    second_half(0)
    block = blocks_of(1)

    pool_a[0:cols, :] = block[0].astype(F32) + block[1].astype(F32)
    small = (pool_a[pl.ds(0, pooled_cols, stride=2), :] + pool_a[pl.ds(1, pooled_cols, stride=2), :]) * 0.25
    keys[me] = small.astype(BF16)
    send_block(keys, 4)

    loads[4].wait()
    loads[5].wait()
    block = blocks_of(0)
    scale = 1.0 / math.sqrt(channels)
    feature = jnp.dot(block.reshape(2 * cols, 128), wp[...], preferred_element_type=F32) + bias[...]
    feature = feature.astype(BF16)
    offset = jnp.sum(feature.astype(F32) * bias[...], axis=1, keepdims=True) * scale
    high, low = split(dot_t(feature, wp[...]) * scale)
    queries = jnp.concatenate([high, low], axis=1)

    query_out[...] = queries
    offset_out[...] = jnp.broadcast_to(offset, offset_out.shape)

    arrived(keys, all_recv.at[4])

    for line in lines:
        slot = line[2]

        @pl.when(inside(line[0], 0))
        def _(slot=slot):
            pltpu.make_async_copy(edge_rows.at[slot], edge_rows.at[slot], row_send.at[slot]).wait()

    for corner in corners:
        slot = corner[3]

        @pl.when(inside(corner[0], corner[1]))
        def _(slot=slot):
            pltpu.make_async_copy(edge_in.at[slot], edge_in.at[slot], edge_send.at[slot]).wait()

    for phase in range(4):
        arrived(stats.at[phase], all_send.at[phase])
    arrived(keys, all_send.at[4])


def correlate(across, keys, query, offset_ref, o1, o2, o3, pool_b, pool_c):
    total_keys = keys.shape[0]
    chunk = min(total_keys, 2048)
    lines1 = chunk // across
    queries = query[...]
    high = queries[:, 0:128]
    offset = offset_ref[:, 0:1]

    def pooled(values, scratch, lines_in, width):
        pairs = jnp.sum(values.reshape(lines_in // 2, 2, width, 128), axis=1)
        count = lines_in // 2 * width
        scratch[0:count, :] = pairs.reshape(count, 128)
        half = count // 2
        return (scratch[pl.ds(0, half, stride=2), :] + scratch[pl.ds(1, half, stride=2), :]) * 0.25

    def fine(values):
        k_high, k_low = split(values)
        return dot_t(queries, jnp.concatenate([k_high, k_high], axis=1)) + dot_t(high, k_low) + offset

    for start in range(0, total_keys, chunk):
        part = keys[start:start + chunk, :]
        level = dot_t(queries, jnp.concatenate([part, part], axis=1)) + offset
        o1[:, start:start + chunk] = level.astype(BF16)
        two = pooled(part.astype(F32), pool_b, lines1, across)
        o2[:, start // 4:(start + chunk) // 4] = fine(two).astype(BF16)
        three = pooled(two, pool_c, lines1 // 2, across // 2)
        o3[:, start // 16:(start + chunk) // 16] = fine(three).astype(BF16)


def body(row_tiles, col_tiles, frame_one, frame_two, first_kernel, second_kernel, out_proj, out_bias):
    rows, cols, cin = frame_one.shape
    channels = out_proj.shape[1]
    devices = row_tiles * col_tiles
    queries = rows * cols
    keys = devices * queries // 4
    wide = cols + 16
    chunk = min(keys, 2048)
    vmem = pltpu.VMEM
    anywhere = pl.BlockSpec(memory_space=pl.ANY)
    local = pl.BlockSpec(memory_space=pltpu.VMEM)
    key_blocks, query, offset = pl.pallas_call(
        functools.partial(kernel, row_tiles, col_tiles, rows, cols),
        out_shape=[
            jax.ShapeDtypeStruct((devices, cols // 2, cin), BF16),
            jax.ShapeDtypeStruct((queries, 2 * cin), BF16),
            jax.ShapeDtypeStruct((queries, 128), F32),
        ],
        in_specs=[anywhere] * 6,
        out_specs=[local] * 3,
        scratch_shapes=[
            vmem((9 * cin, cin), BF16),
            vmem((9 * cin, cin), BF16),
            vmem((cin, channels), BF16),
            vmem((1, channels), F32),
            vmem((2, rows, cols, cin), BF16),
            vmem((4, 2, cols, cin), BF16),
            vmem((2, 8, cin), F32),
            vmem((6, 8, cin), F32),
            vmem((2, 6, cols + 32, cin), F32),
            vmem((2, 6, wide, 3 * cin), BF16),
            vmem((2, 4, wide, cin), F32),
            vmem((2, 4, cols + 32, cin), F32),
            vmem((2, 4, cols, 3 * cin), BF16),
            vmem((2, rows, cols, cin), F32),
            vmem((4, devices, 2, cin), F32),
            vmem((cols, cin), F32),
            pltpu.SemaphoreType.DMA((6,)),
            pltpu.SemaphoreType.DMA((4,)),
            pltpu.SemaphoreType.DMA((4,)),
            pltpu.SemaphoreType.DMA((6,)),
            pltpu.SemaphoreType.DMA((6,)),
            pltpu.SemaphoreType.DMA((5,)),
            pltpu.SemaphoreType.DMA((5,)),
        ],
        compiler_params=pltpu.CompilerParams(
            collective_id=0, has_side_effects=True, vmem_limit_bytes=48 * 1024 * 1024
        ),
    )(*[
        pltpu.with_memory_space_constraint(value, pltpu.HBM)
        for value in (
            frame_one, frame_two,
            first_kernel.reshape(9 * cin, cin), second_kernel.reshape(9 * cin, cin),
            out_proj, out_bias.reshape(1, channels),
        )
    ])
    outs = pl.pallas_call(
        functools.partial(correlate, col_tiles * cols // 2),
        out_shape=[
            jax.ShapeDtypeStruct((queries, keys), BF16),
            jax.ShapeDtypeStruct((queries, keys // 4), BF16),
            jax.ShapeDtypeStruct((queries, keys // 16), BF16),
        ],
        in_specs=[local] * 3,
        out_specs=[local] * 3,
        scratch_shapes=[vmem((chunk // 2, cin), F32), vmem((chunk // 8, cin), F32)],
        compiler_params=pltpu.CompilerParams(vmem_limit_bytes=24 * 1024 * 1024),
    )(key_blocks.reshape(keys, cin), query, offset)
    return tuple(out.reshape(rows, cols, -1) for out in outs)


def solution(mesh):
    in_specs = (P("tr", "tc", None), P("tr", "tc", None), P(), P(), P(), P())
    out_specs = (P("tr", "tc", None), P("tr", "tc", None), P("tr", "tc", None))
    step = functools.partial(body, mesh.shape["tr"], mesh.shape["tc"])
    return jax.shard_map(step, mesh=mesh, in_specs=in_specs, out_specs=out_specs, check_vma=False)
```

```python
import functools
import math

import jax
import jax.numpy as jnp
from jax import lax
from jax.experimental import pallas as pl
from jax.experimental.pallas import tpu as pltpu
from jax.sharding import PartitionSpec as P

MESH = pl.DeviceIdType.MESH
FLAT = pl.DeviceIdType.LOGICAL
F32 = jnp.float32
BF16 = jnp.bfloat16


def dot_t(a, b):
    return lax.dot_general(a, b, (((1,), (1,)), ((), ())), preferred_element_type=F32)


def split(values):
    high = values.astype(BF16)
    low = (values - high.astype(F32)).astype(BF16)
    return high, low


def kernel(
    row_tiles, col_tiles, rows, cols,
    f1, f2, w1_hbm, w2_hbm, wp_hbm, bias_hbm,
    keys, query_out, offset_out,
    w1, w2, wp, bias,
    tiles, edge_rows, edge_out, edge_in,
    grid, patches, conv, hidden, patches2, conv2,
    stats, pool_a,
    in_sem, row_send, row_recv, edge_send, edge_recv, all_send, all_recv, key_recv,
):
    tr = lax.axis_index("tr")
    tc = lax.axis_index("tc")
    devices = row_tiles * col_tiles
    me = tr * col_tiles + tc
    positions = float(devices * rows * cols)
    channels = wp.shape[1]
    pooled_cols = cols // 2

    loads = [
        pltpu.make_async_copy(f1, tiles.at[0], in_sem.at[0]),
        pltpu.make_async_copy(f2, tiles.at[1], in_sem.at[1]),
        pltpu.make_async_copy(w1_hbm, w1, in_sem.at[2]),
        pltpu.make_async_copy(w2_hbm, w2, in_sem.at[3]),
        pltpu.make_async_copy(wp_hbm, wp, in_sem.at[4]),
        pltpu.make_async_copy(bias_hbm, bias, in_sem.at[5]),
    ]
    for load in loads:
        load.start()

    edge_rows[...] = jnp.zeros_like(edge_rows)
    edge_in[...] = jnp.zeros_like(edge_in)

    def inside(down, side):
        row = tr + down
        col = tc + side
        return (row >= 0) & (row < row_tiles) & (col >= 0) & (col < col_tiles)

    far_first = sorted(range(1, devices), key=lambda s: -min(s, devices - s))
    close = (1, col_tiles - 1, col_tiles, col_tiles + 1)
    close_first = sorted(far_first, key=lambda s: min(s, devices - s) not in close)

    def wrap(index):
        return jnp.where(index < devices, index, index - devices)

    def each(act, order):
        def turn(step, carried=0):
            act(wrap(me + step))
            return carried

        if devices <= 32:
            for step in order:
                turn(step)
        else:
            lax.fori_loop(1, devices, turn, 0)

    barrier = pltpu.get_barrier_semaphore()

    def greet(index):
        pl.semaphore_signal(barrier, inc=1, device_id=index, device_id_type=FLAT)

    each(greet, close_first)

    loads[0].wait()
    loads[1].wait()
    left = 16
    right = left + cols
    for f in range(2):
        for y in range(2):
            values = tiles[f, y].astype(F32)
            grid[f, 2 + y, left:right, :] = values
            line = f * 4 + y * 2
            edge_out[0, line:line + 2, :] = values[0:2]
            edge_out[1, line:line + 2, :] = values[cols - 2:cols]

    pl.semaphore_wait(barrier, devices - 1)

    corners = [
        (0, 1, 1, 0), (0, -1, 0, 1),
        (1, 1, 1, 2), (1, -1, 0, 3),
        (-1, 1, 1, 4), (-1, -1, 0, 5),
    ]
    lines = [(1, 1, 0), (-1, 0, 1), (1, 0, 2), (-1, 1, 3)]

    def row_copy(f, down, row, slot):
        return pltpu.make_async_remote_copy(
            src_ref=tiles.at[f, row], dst_ref=edge_rows.at[slot, f],
            send_sem=row_send.at[slot, f], recv_sem=row_recv.at[slot, f],
            device_id=(tr + down, tc), device_id_type=MESH,
        )

    def edge_copy(down, side, which, slot):
        return pltpu.make_async_remote_copy(
            src_ref=edge_out.at[which], dst_ref=edge_in.at[slot],
            send_sem=edge_send.at[slot], recv_sem=edge_recv.at[slot],
            device_id=(tr + down, tc + side), device_id_type=MESH,
        )

    def send_row(f, line):
        @pl.when(inside(line[0], 0))
        def _():
            row_copy(f, *line).start()

    def send_edge(corner):
        @pl.when(inside(corner[0], corner[1]))
        def _():
            edge_copy(*corner).start()

    def await_row(f, line):
        landed = edge_rows.at[line[2], f]

        @pl.when(inside(-line[0], 0))
        def _():
            pltpu.make_async_copy(landed, landed, row_recv.at[line[2], f]).wait()

    def await_edge(corner):
        slot = corner[3]

        @pl.when(inside(-corner[0], -corner[1]))
        def _():
            pltpu.make_async_copy(edge_in.at[slot], edge_in.at[slot], edge_recv.at[slot]).wait()

    for corner in corners:
        send_edge(corner)
    for pair in (lines[:2], lines[2:]):
        for f in (1, 0):
            for line in pair:
                send_row(f, line)

    wide = cols + 16

    def fill_row(f, y, slot):
        grid[f, y, left:right, :] = edge_rows[slot, f].astype(F32)

    def fill_edges(f, y, slot, base):
        line = f * 4 + base * 2
        grid[f, y, left - 2:left, :] = edge_in[slot, line:line + 2, :]
        grid[f, y, right:right + 2, :] = edge_in[slot + 1, line:line + 2, :]

    def fill_patches(f, y):
        for j in range(3):
            start = left - 9 + j
            patches[f, y, :, j * 128:(j + 1) * 128] = grid[f, y, start:start + wide, :].astype(BF16)

    def patch(source, f, *lines_in):
        return jnp.concatenate([source[f, y] for y in lines_in], axis=1)

    def times(window, weights):
        return jnp.dot(window, weights, preferred_element_type=F32)

    def middle(weights):
        return jnp.concatenate([weights[384:1152], weights[0:768]], axis=1)

    def send_block(slots, phase):
        each(lambda index: pltpu.make_async_remote_copy(
            src_ref=slots.at[me], dst_ref=slots.at[me],
            send_sem=all_send.at[phase], recv_sem=all_recv.at[phase],
            device_id=index, device_id_type=FLAT,
        ).start(), far_first)

    def arrived(slots, sem):
        others = slots.at[pl.ds(0, devices - 1)]
        pltpu.make_async_copy(others, others, sem).wait()

    def share(upper, lower, phase):
        total = jnp.sum(upper + lower, axis=0, keepdims=True)
        squares = jnp.sum(upper * upper + lower * lower, axis=0, keepdims=True)
        stats[phase, me] = jnp.concatenate([total, squares], axis=0)
        send_block(stats.at[phase], phase)

    def collect(phase):
        arrived(stats.at[phase], all_recv.at[phase])
        total = jnp.sum(stats[phase], axis=0) / positions
        centre = total[0:1]
        spread = total[1:2] - centre * centre
        return centre, lax.rsqrt(spread + 1e-05)

    spot = lax.broadcasted_iota(jnp.int32, (wide, 128), 0)
    col_ok = ((spot >= 8) | (tc > 0)) & ((spot < 8 + cols) | (tc < col_tiles - 1))
    row_ok = (col_ok & (tr > 0), col_ok, col_ok, col_ok & (tr < row_tiles - 1))

    def start_own(f):
        for y in range(2):
            fill_edges(f, 2 + y, 0, y)
            fill_patches(f, 2 + y)
        return times(patch(patches, f, 2, 3), middle(w1))

    def finish_own(f, both):
        fill_row(f, 1, 0)
        fill_row(f, 4, 1)
        for y in range(2):
            fill_edges(f, 0 + y, 2, y)
            fill_edges(f, 4 + y, 4, y)
        fill_patches(f, 1)
        fill_patches(f, 4)
        conv[f, 1] = both[:, 0:128] + times(patches[f, 1], w1[0:384])
        conv[f, 2] = both[:, 128:256] + times(patches[f, 4], w1[768:1152])
        share(conv[f, 1, 8:8 + cols], conv[f, 2, 8:8 + cols], f)

    def edge_lines(f):
        fill_row(f, 0, 2)
        fill_row(f, 5, 3)
        fill_patches(f, 0)
        fill_patches(f, 5)
        conv[f, 0] = times(patch(patches, f, 0, 1, 2), w1[...])
        conv[f, 3] = times(patch(patches, f, 3, 4, 5), w1[...])

    def second_half(f):
        centre, inverse = collect(f)
        for y in range(4):
            values = jax.nn.relu((conv[f, y] - centre) * inverse)
            hidden[f, y, 8:8 + wide, :] = jnp.where(row_ok[y], values, 0.0)
            for j in range(3):
                start = left - 1 + j
                patches2[f, y, :, j * 128:(j + 1) * 128] = hidden[f, y, start:start + cols, :].astype(BF16)
        both = times(patch(patches2, f, 1, 2), middle(w2))
        upper = both[:, 0:128] + times(patches2[f, 0], w2[0:384])
        lower = both[:, 128:256] + times(patches2[f, 3], w2[768:1152])
        share(upper, lower, 2 + f)
        conv2[f, 0] = upper
        conv2[f, 1] = lower

    def blocks_of(f):
        centre, inverse = collect(2 + f)
        values = jax.nn.relu((conv2[f] - centre) * inverse)
        return jax.nn.relu(tiles[f].astype(F32) + values).astype(BF16)

    for corner in corners[:2]:
        await_edge(corner)
    loads[2].wait()
    both = start_own(1)
    for line in lines[:2]:
        await_row(1, line)
    for corner in corners[2:]:
        await_edge(corner)
    finish_own(1, both)
    both = start_own(0)
    for line in lines[:2]:
        await_row(0, line)
    finish_own(0, both)
    for line in lines[2:]:
        await_row(1, line)
    edge_lines(1)
    loads[3].wait()
    second_half(1)
    for line in lines[2:]:
        await_row(0, line)
    edge_lines(0)
    second_half(0)
    block = blocks_of(1)

    pool_a[0:cols, :] = block[0].astype(F32) + block[1].astype(F32)
    small = (pool_a[pl.ds(0, pooled_cols, stride=2), :] + pool_a[pl.ds(1, pooled_cols, stride=2), :]) * 0.25
    keys[me] = small.astype(BF16)
    sibling = jnp.where(lax.rem(tc, 2) == 0, me + 1, me - 1)
    chips = devices // 2

    def hand_over(block):
        pltpu.make_async_remote_copy(
            src_ref=keys.at[block], dst_ref=keys.at[block],
            send_sem=all_send.at[5], recv_sem=all_recv.at[5],
            device_id=sibling, device_id_type=FLAT,
        ).start()

    def send_key(hop):
        pltpu.make_async_remote_copy(
            src_ref=keys.at[me], dst_ref=keys.at[me],
            send_sem=all_send.at[4], recv_sem=key_recv.at[hop],
            device_id=wrap(me + 2 * hop), device_id_type=FLAT,
        ).start()

    def pass_key(hop):
        block = wrap(me + devices - 2 * hop)
        pltpu.make_async_copy(keys.at[block], keys.at[block], key_recv.at[hop]).wait()
        hand_over(block)

    def each_chip(act, order):
        def turn(hop, carried=0):
            act(hop)
            return carried

        if chips <= 16:
            for hop in order:
                turn(hop)
        else:
            lax.fori_loop(1, chips, turn, 0)

    far_chips = sorted(range(1, chips), key=lambda h: -min(h, chips - h))
    each_chip(send_key, far_chips)
    hand_over(me)

    loads[4].wait()
    loads[5].wait()
    block = blocks_of(0)
    scale = 1.0 / math.sqrt(channels)
    feature = jnp.dot(block.reshape(2 * cols, 128), wp[...], preferred_element_type=F32) + bias[...]
    feature = feature.astype(BF16)
    offset = jnp.sum(feature.astype(F32) * bias[...], axis=1, keepdims=True) * scale
    high, low = split(dot_t(feature, wp[...]) * scale)
    queries = jnp.concatenate([high, low], axis=1)

    query_out[...] = queries
    offset_out[...] = jnp.broadcast_to(offset, offset_out.shape)

    each_chip(pass_key, far_chips[::-1])
    handed = keys.at[pl.ds(0, chips)]
    pltpu.make_async_copy(handed, handed, all_recv.at[5]).wait()

    for line in lines:
        for f in range(2):
            @pl.when(inside(line[0], 0))
            def _(slot=line[2], f=f):
                gone = edge_rows.at[slot, f]
                pltpu.make_async_copy(gone, gone, row_send.at[slot, f]).wait()

    for corner in corners:
        slot = corner[3]

        @pl.when(inside(corner[0], corner[1]))
        def _(slot=slot):
            pltpu.make_async_copy(edge_in.at[slot], edge_in.at[slot], edge_send.at[slot]).wait()

    for phase in range(4):
        arrived(stats.at[phase], all_send.at[phase])
    sent = keys.at[pl.ds(0, chips - 1)]
    pltpu.make_async_copy(sent, sent, all_send.at[4]).wait()
    pltpu.make_async_copy(handed, handed, all_send.at[5]).wait()


def correlate(across, keys, query, offset_ref, o1, o2, o3, pool_b, pool_c):
    total_keys = keys.shape[0]
    chunk = min(total_keys, 2048)
    lines1 = chunk // across
    queries = query[...]
    high = queries[:, 0:128]
    offset = offset_ref[:, 0:1]

    def pooled(values, scratch, lines_in, width):
        pairs = jnp.sum(values.reshape(lines_in // 2, 2, width, 128), axis=1)
        count = lines_in // 2 * width
        scratch[0:count, :] = pairs.reshape(count, 128)
        half = count // 2
        return (scratch[pl.ds(0, half, stride=2), :] + scratch[pl.ds(1, half, stride=2), :]) * 0.25

    def fine(values):
        k_high, k_low = split(values)
        return dot_t(queries, jnp.concatenate([k_high, k_high], axis=1)) + dot_t(high, k_low) + offset

    for start in range(0, total_keys, chunk):
        part = keys[start:start + chunk, :]
        level = dot_t(queries, jnp.concatenate([part, part], axis=1)) + offset
        o1[:, start:start + chunk] = level.astype(BF16)
        two = pooled(part.astype(F32), pool_b, lines1, across)
        o2[:, start // 4:(start + chunk) // 4] = fine(two).astype(BF16)
        three = pooled(two, pool_c, lines1 // 2, across // 2)
        o3[:, start // 16:(start + chunk) // 16] = fine(three).astype(BF16)


def body(row_tiles, col_tiles, frame_one, frame_two, first_kernel, second_kernel, out_proj, out_bias):
    rows, cols, cin = frame_one.shape
    channels = out_proj.shape[1]
    devices = row_tiles * col_tiles
    queries = rows * cols
    keys = devices * queries // 4
    wide = cols + 16
    chunk = min(keys, 2048)
    vmem = pltpu.VMEM
    anywhere = pl.BlockSpec(memory_space=pl.ANY)
    local = pl.BlockSpec(memory_space=pltpu.VMEM)
    key_blocks, query, offset = pl.pallas_call(
        functools.partial(kernel, row_tiles, col_tiles, rows, cols),
        out_shape=[
            jax.ShapeDtypeStruct((devices, cols // 2, cin), BF16),
            jax.ShapeDtypeStruct((queries, 2 * cin), BF16),
            jax.ShapeDtypeStruct((queries, 128), F32),
        ],
        in_specs=[anywhere] * 6,
        out_specs=[local] * 3,
        scratch_shapes=[
            vmem((9 * cin, cin), BF16),
            vmem((9 * cin, cin), BF16),
            vmem((cin, channels), BF16),
            vmem((1, channels), F32),
            vmem((2, rows, cols, cin), BF16),
            vmem((4, 2, cols, cin), BF16),
            vmem((2, 8, cin), F32),
            vmem((6, 8, cin), F32),
            vmem((2, 6, cols + 32, cin), F32),
            vmem((2, 6, wide, 3 * cin), BF16),
            vmem((2, 4, wide, cin), F32),
            vmem((2, 4, cols + 32, cin), F32),
            vmem((2, 4, cols, 3 * cin), BF16),
            vmem((2, rows, cols, cin), F32),
            vmem((4, devices, 2, cin), F32),
            vmem((cols, cin), F32),
            pltpu.SemaphoreType.DMA((6,)),
            pltpu.SemaphoreType.DMA((4, 2)),
            pltpu.SemaphoreType.DMA((4, 2)),
            pltpu.SemaphoreType.DMA((6,)),
            pltpu.SemaphoreType.DMA((6,)),
            pltpu.SemaphoreType.DMA((6,)),
            pltpu.SemaphoreType.DMA((6,)),
            pltpu.SemaphoreType.DMA((devices // 2,)),
        ],
        compiler_params=pltpu.CompilerParams(
            collective_id=0, has_side_effects=True, vmem_limit_bytes=48 * 1024 * 1024
        ),
    )(*[
        pltpu.with_memory_space_constraint(value, pltpu.HBM)
        for value in (
            frame_one, frame_two,
            first_kernel.reshape(9 * cin, cin), second_kernel.reshape(9 * cin, cin),
            out_proj, out_bias.reshape(1, channels),
        )
    ])
    outs = pl.pallas_call(
        functools.partial(correlate, col_tiles * cols // 2),
        out_shape=[
            jax.ShapeDtypeStruct((queries, keys), BF16),
            jax.ShapeDtypeStruct((queries, keys // 4), BF16),
            jax.ShapeDtypeStruct((queries, keys // 16), BF16),
        ],
        in_specs=[local] * 3,
        out_specs=[local] * 3,
        scratch_shapes=[vmem((chunk // 2, cin), F32), vmem((chunk // 8, cin), F32)],
        compiler_params=pltpu.CompilerParams(vmem_limit_bytes=24 * 1024 * 1024),
    )(key_blocks.reshape(keys, cin), query, offset)
    return tuple(out.reshape(rows, cols, -1) for out in outs)


def solution(mesh):
    in_specs = (P("tr", "tc", None), P("tr", "tc", None), P(), P(), P(), P())
    out_specs = (P("tr", "tc", None), P("tr", "tc", None), P("tr", "tc", None))
    step = functools.partial(body, mesh.shape["tr"], mesh.shape["tc"])
    return jax.shard_map(step, mesh=mesh, in_specs=in_specs, out_specs=out_specs, check_vma=False)
```

```python
import functools
import math

import jax
import jax.numpy as jnp
from jax import lax
from jax.experimental import pallas as pl
from jax.experimental.pallas import tpu as pltpu
from jax.sharding import PartitionSpec as P

MESH = pl.DeviceIdType.MESH
FLAT = pl.DeviceIdType.LOGICAL
F32 = jnp.float32
BF16 = jnp.bfloat16


def dot_t(a, b):
    return lax.dot_general(a, b, (((1,), (1,)), ((), ())), preferred_element_type=F32)


def split(values):
    high = values.astype(BF16)
    low = (values - high.astype(F32)).astype(BF16)
    return high, low


def kernel(
    row_tiles, col_tiles, rows, cols,
    f1, f2, w1_hbm, w2_hbm, wp_hbm, bias_hbm,
    keys, query_out, offset_out,
    w1, w2, wp, bias,
    tiles, edge_rows, edge_out, edge_in,
    grid, patches, conv, hidden, patches2, conv2,
    stats, pool_a,
    in_sem, row_send, row_recv, edge_send, edge_recv, all_send, all_recv, key_recv,
):
    tr = lax.axis_index("tr")
    tc = lax.axis_index("tc")
    devices = row_tiles * col_tiles
    me = tr * col_tiles + tc
    positions = float(devices * rows * cols)
    channels = wp.shape[1]
    pooled_cols = cols // 2

    loads = [
        pltpu.make_async_copy(f1, tiles.at[0], in_sem.at[0]),
        pltpu.make_async_copy(f2, tiles.at[1], in_sem.at[1]),
        pltpu.make_async_copy(w1_hbm, w1, in_sem.at[2]),
        pltpu.make_async_copy(w2_hbm, w2, in_sem.at[3]),
        pltpu.make_async_copy(wp_hbm, wp, in_sem.at[4]),
        pltpu.make_async_copy(bias_hbm, bias, in_sem.at[5]),
    ]
    for load in loads:
        load.start()

    edge_rows[...] = jnp.zeros_like(edge_rows)
    edge_in[...] = jnp.zeros_like(edge_in)

    def inside(down, side):
        row = tr + down
        col = tc + side
        return (row >= 0) & (row < row_tiles) & (col >= 0) & (col < col_tiles)

    def wrap(index):
        return jnp.where(index < devices, index, index - devices)

    def around(count, act, near):
        half = count // 2

        def turn(turn_index, carried):
            step = turn_index if near else half - turn_index
            act(step)
            act(count - step)
            return carried

        if not near:
            act(half)
        lax.fori_loop(1, half, turn, 0)
        if near:
            act(half)

    def each(act, near=False):
        around(devices, lambda step: act(wrap(me + step)), near)

    barrier = pltpu.get_barrier_semaphore()

    def greet(index):
        pl.semaphore_signal(barrier, inc=1, device_id=index, device_id_type=FLAT)

    each(greet, near=True)

    loads[0].wait()
    loads[1].wait()
    left = 16
    right = left + cols
    for f in range(2):
        for y in range(2):
            values = tiles[f, y].astype(F32)
            grid[f, 2 + y, left:right, :] = values
            line = f * 4 + y * 2
            edge_out[0, line:line + 2, :] = values[0:2]
            edge_out[1, line:line + 2, :] = values[cols - 2:cols]

    pl.semaphore_wait(barrier, devices - 1)

    corners = [
        (0, 1, 1, 0), (0, -1, 0, 1),
        (1, 1, 1, 2), (1, -1, 0, 3),
        (-1, 1, 1, 4), (-1, -1, 0, 5),
    ]
    lines = [(1, 1, 0), (-1, 0, 1), (1, 0, 2), (-1, 1, 3)]

    def row_copy(f, down, row, slot):
        return pltpu.make_async_remote_copy(
            src_ref=tiles.at[f, row], dst_ref=edge_rows.at[slot, f],
            send_sem=row_send.at[slot, f], recv_sem=row_recv.at[slot, f],
            device_id=(tr + down, tc), device_id_type=MESH,
        )

    def edge_copy(down, side, which, slot):
        return pltpu.make_async_remote_copy(
            src_ref=edge_out.at[which], dst_ref=edge_in.at[slot],
            send_sem=edge_send.at[slot], recv_sem=edge_recv.at[slot],
            device_id=(tr + down, tc + side), device_id_type=MESH,
        )

    def send_row(f, line):
        @pl.when(inside(line[0], 0))
        def _():
            row_copy(f, *line).start()

    def send_edge(corner):
        @pl.when(inside(corner[0], corner[1]))
        def _():
            edge_copy(*corner).start()

    def await_row(f, line):
        landed = edge_rows.at[line[2], f]

        @pl.when(inside(-line[0], 0))
        def _():
            pltpu.make_async_copy(landed, landed, row_recv.at[line[2], f]).wait()

    def await_edge(corner):
        slot = corner[3]

        @pl.when(inside(-corner[0], -corner[1]))
        def _():
            pltpu.make_async_copy(edge_in.at[slot], edge_in.at[slot], edge_recv.at[slot]).wait()

    for corner in corners:
        send_edge(corner)
    for pair in (lines[:2], lines[2:]):
        for f in (1, 0):
            for line in pair:
                send_row(f, line)

    wide = cols + 16

    def fill_row(f, y, slot):
        grid[f, y, left:right, :] = edge_rows[slot, f].astype(F32)

    def fill_edges(f, y, slot, base):
        line = f * 4 + base * 2
        grid[f, y, left - 2:left, :] = edge_in[slot, line:line + 2, :]
        grid[f, y, right:right + 2, :] = edge_in[slot + 1, line:line + 2, :]

    def fill_patches(f, y):
        for j in range(3):
            start = left - 9 + j
            patches[f, y, :, j * 128:(j + 1) * 128] = grid[f, y, start:start + wide, :].astype(BF16)

    def patch(source, f, *lines_in):
        return jnp.concatenate([source[f, y] for y in lines_in], axis=1)

    def times(window, weights):
        return jnp.dot(window, weights, preferred_element_type=F32)

    def middle(weights):
        return jnp.concatenate([weights[384:1152], weights[0:768]], axis=1)

    def send_block(slots, phase):
        each(lambda index: pltpu.make_async_remote_copy(
            src_ref=slots.at[me], dst_ref=slots.at[me],
            send_sem=all_send.at[phase], recv_sem=all_recv.at[phase],
            device_id=index, device_id_type=FLAT,
        ).start())

    def arrived(slots, sem):
        others = slots.at[pl.ds(0, devices - 1)]
        pltpu.make_async_copy(others, others, sem).wait()

    def share(upper, lower, phase):
        total = jnp.sum(upper + lower, axis=0, keepdims=True)
        squares = jnp.sum(upper * upper + lower * lower, axis=0, keepdims=True)
        stats[phase, me] = jnp.concatenate([total, squares], axis=0)
        send_block(stats.at[phase], phase)

    def collect(phase):
        arrived(stats.at[phase], all_recv.at[phase])
        total = jnp.sum(stats[phase], axis=0) / positions
        centre = total[0:1]
        spread = total[1:2] - centre * centre
        return centre, lax.rsqrt(spread + 1e-05)

    spot = lax.broadcasted_iota(jnp.int32, (wide, 128), 0)
    col_ok = ((spot >= 8) | (tc > 0)) & ((spot < 8 + cols) | (tc < col_tiles - 1))
    row_ok = (col_ok & (tr > 0), col_ok, col_ok, col_ok & (tr < row_tiles - 1))

    def start_own(f):
        for y in range(2):
            fill_edges(f, 2 + y, 0, y)
            fill_patches(f, 2 + y)
        return times(patch(patches, f, 2, 3), middle(w1))

    def finish_own(f, both):
        fill_row(f, 1, 0)
        fill_row(f, 4, 1)
        for y in range(2):
            fill_edges(f, 0 + y, 2, y)
            fill_edges(f, 4 + y, 4, y)
        fill_patches(f, 1)
        fill_patches(f, 4)
        conv[f, 1] = both[:, 0:128] + times(patches[f, 1], w1[0:384])
        conv[f, 2] = both[:, 128:256] + times(patches[f, 4], w1[768:1152])
        share(conv[f, 1, 8:8 + cols], conv[f, 2, 8:8 + cols], f)

    def edge_lines(f):
        fill_row(f, 0, 2)
        fill_row(f, 5, 3)
        fill_patches(f, 0)
        fill_patches(f, 5)
        conv[f, 0] = times(patch(patches, f, 0, 1, 2), w1[...])
        conv[f, 3] = times(patch(patches, f, 3, 4, 5), w1[...])

    def second_half(f):
        centre, inverse = collect(f)
        for y in range(4):
            values = jax.nn.relu((conv[f, y] - centre) * inverse)
            hidden[f, y, 8:8 + wide, :] = jnp.where(row_ok[y], values, 0.0)
            for j in range(3):
                start = left - 1 + j
                patches2[f, y, :, j * 128:(j + 1) * 128] = hidden[f, y, start:start + cols, :].astype(BF16)
        both = times(patch(patches2, f, 1, 2), middle(w2))
        upper = both[:, 0:128] + times(patches2[f, 0], w2[0:384])
        lower = both[:, 128:256] + times(patches2[f, 3], w2[768:1152])
        share(upper, lower, 2 + f)
        conv2[f, 0] = upper
        conv2[f, 1] = lower

    def blocks_of(f):
        centre, inverse = collect(2 + f)
        values = jax.nn.relu((conv2[f] - centre) * inverse)
        return jax.nn.relu(tiles[f].astype(F32) + values).astype(BF16)

    for corner in corners[:2]:
        await_edge(corner)
    loads[2].wait()
    both = start_own(1)
    for line in lines[:2]:
        await_row(1, line)
    for corner in corners[2:]:
        await_edge(corner)
    finish_own(1, both)
    both = start_own(0)
    for line in lines[:2]:
        await_row(0, line)
    finish_own(0, both)
    for line in lines[2:]:
        await_row(1, line)
    edge_lines(1)
    loads[3].wait()
    second_half(1)
    for line in lines[2:]:
        await_row(0, line)
    edge_lines(0)
    second_half(0)
    block = blocks_of(1)

    pool_a[0:cols, :] = block[0].astype(F32) + block[1].astype(F32)
    small = (pool_a[pl.ds(0, pooled_cols, stride=2), :] + pool_a[pl.ds(1, pooled_cols, stride=2), :]) * 0.25
    keys[me] = small.astype(BF16)
    sibling = jnp.where(lax.rem(tc, 2) == 0, me + 1, me - 1)
    chips = devices // 2

    def hand_over(block):
        pltpu.make_async_remote_copy(
            src_ref=keys.at[block], dst_ref=keys.at[block],
            send_sem=all_send.at[5], recv_sem=all_recv.at[5],
            device_id=sibling, device_id_type=FLAT,
        ).start()

    def send_key(hop):
        pltpu.make_async_remote_copy(
            src_ref=keys.at[me], dst_ref=keys.at[me],
            send_sem=all_send.at[4], recv_sem=key_recv.at[hop],
            device_id=wrap(me + 2 * hop), device_id_type=FLAT,
        ).start()

    def pass_key(hop):
        block = wrap(me + devices - 2 * hop)
        pltpu.make_async_copy(keys.at[block], keys.at[block], key_recv.at[hop]).wait()
        hand_over(block)

    around(chips, send_key, near=False)
    hand_over(me)

    loads[4].wait()
    loads[5].wait()
    block = blocks_of(0)
    scale = 1.0 / math.sqrt(channels)
    feature = jnp.dot(block.reshape(2 * cols, 128), wp[...], preferred_element_type=F32) + bias[...]
    feature = feature.astype(BF16)
    offset = jnp.sum(feature.astype(F32) * bias[...], axis=1, keepdims=True) * scale
    high, low = split(dot_t(feature, wp[...]) * scale)
    queries = jnp.concatenate([high, low], axis=1)

    query_out[...] = queries
    offset_out[...] = jnp.broadcast_to(offset, offset_out.shape)

    around(chips, pass_key, near=True)
    handed = keys.at[pl.ds(0, chips)]
    pltpu.make_async_copy(handed, handed, all_recv.at[5]).wait()

    for line in lines:
        for f in range(2):
            @pl.when(inside(line[0], 0))
            def _(slot=line[2], f=f):
                gone = edge_rows.at[slot, f]
                pltpu.make_async_copy(gone, gone, row_send.at[slot, f]).wait()

    for corner in corners:
        slot = corner[3]

        @pl.when(inside(corner[0], corner[1]))
        def _(slot=slot):
            pltpu.make_async_copy(edge_in.at[slot], edge_in.at[slot], edge_send.at[slot]).wait()

    for phase in range(4):
        arrived(stats.at[phase], all_send.at[phase])
    sent = keys.at[pl.ds(0, chips - 1)]
    pltpu.make_async_copy(sent, sent, all_send.at[4]).wait()
    pltpu.make_async_copy(handed, handed, all_send.at[5]).wait()


def correlate(across, keys, query, offset_ref, o1, o2, o3, pool_b, pool_c):
    total_keys = keys.shape[0]
    chunk = min(total_keys, 2048)
    lines1 = chunk // across
    queries = query[...]
    high = queries[:, 0:128]
    offset = offset_ref[:, 0:1]

    def pooled(values, scratch, lines_in, width):
        pairs = jnp.sum(values.reshape(lines_in // 2, 2, width, 128), axis=1)
        count = lines_in // 2 * width
        scratch[0:count, :] = pairs.reshape(count, 128)
        half = count // 2
        return (scratch[pl.ds(0, half, stride=2), :] + scratch[pl.ds(1, half, stride=2), :]) * 0.25

    def fine(values):
        k_high, k_low = split(values)
        return dot_t(queries, jnp.concatenate([k_high, k_high], axis=1)) + dot_t(high, k_low) + offset

    for start in range(0, total_keys, chunk):
        part = keys[start:start + chunk, :]
        level = dot_t(queries, jnp.concatenate([part, part], axis=1)) + offset
        o1[:, start:start + chunk] = level.astype(BF16)
        two = pooled(part.astype(F32), pool_b, lines1, across)
        o2[:, start // 4:(start + chunk) // 4] = fine(two).astype(BF16)
        three = pooled(two, pool_c, lines1 // 2, across // 2)
        o3[:, start // 16:(start + chunk) // 16] = fine(three).astype(BF16)


def body(row_tiles, col_tiles, frame_one, frame_two, first_kernel, second_kernel, out_proj, out_bias):
    rows, cols, cin = frame_one.shape
    channels = out_proj.shape[1]
    devices = row_tiles * col_tiles
    queries = rows * cols
    keys = devices * queries // 4
    wide = cols + 16
    chunk = min(keys, 2048)
    vmem = pltpu.VMEM
    anywhere = pl.BlockSpec(memory_space=pl.ANY)
    local = pl.BlockSpec(memory_space=pltpu.VMEM)
    key_blocks, query, offset = pl.pallas_call(
        functools.partial(kernel, row_tiles, col_tiles, rows, cols),
        out_shape=[
            jax.ShapeDtypeStruct((devices, cols // 2, cin), BF16),
            jax.ShapeDtypeStruct((queries, 2 * cin), BF16),
            jax.ShapeDtypeStruct((queries, 128), F32),
        ],
        in_specs=[anywhere] * 6,
        out_specs=[local] * 3,
        scratch_shapes=[
            vmem((9 * cin, cin), BF16),
            vmem((9 * cin, cin), BF16),
            vmem((cin, channels), BF16),
            vmem((1, channels), F32),
            vmem((2, rows, cols, cin), BF16),
            vmem((4, 2, cols, cin), BF16),
            vmem((2, 8, cin), F32),
            vmem((6, 8, cin), F32),
            vmem((2, 6, cols + 32, cin), F32),
            vmem((2, 6, wide, 3 * cin), BF16),
            vmem((2, 4, wide, cin), F32),
            vmem((2, 4, cols + 32, cin), F32),
            vmem((2, 4, cols, 3 * cin), BF16),
            vmem((2, rows, cols, cin), F32),
            vmem((4, devices, 2, cin), F32),
            vmem((cols, cin), F32),
            pltpu.SemaphoreType.DMA((6,)),
            pltpu.SemaphoreType.DMA((4, 2)),
            pltpu.SemaphoreType.DMA((4, 2)),
            pltpu.SemaphoreType.DMA((6,)),
            pltpu.SemaphoreType.DMA((6,)),
            pltpu.SemaphoreType.DMA((6,)),
            pltpu.SemaphoreType.DMA((6,)),
            pltpu.SemaphoreType.DMA((devices // 2,)),
        ],
        compiler_params=pltpu.CompilerParams(
            collective_id=0, has_side_effects=True, vmem_limit_bytes=48 * 1024 * 1024
        ),
    )(*[
        pltpu.with_memory_space_constraint(value, pltpu.HBM)
        for value in (
            frame_one, frame_two,
            first_kernel.reshape(9 * cin, cin), second_kernel.reshape(9 * cin, cin),
            out_proj, out_bias.reshape(1, channels),
        )
    ])
    outs = pl.pallas_call(
        functools.partial(correlate, col_tiles * cols // 2),
        out_shape=[
            jax.ShapeDtypeStruct((queries, keys), BF16),
            jax.ShapeDtypeStruct((queries, keys // 4), BF16),
            jax.ShapeDtypeStruct((queries, keys // 16), BF16),
        ],
        in_specs=[local] * 3,
        out_specs=[local] * 3,
        scratch_shapes=[vmem((chunk // 2, cin), F32), vmem((chunk // 8, cin), F32)],
        compiler_params=pltpu.CompilerParams(vmem_limit_bytes=24 * 1024 * 1024),
    )(key_blocks.reshape(keys, cin), query, offset)
    return tuple(out.reshape(rows, cols, -1) for out in outs)


def solution(mesh):
    in_specs = (P("tr", "tc", None), P("tr", "tc", None), P(), P(), P(), P())
    out_specs = (P("tr", "tc", None), P("tr", "tc", None), P("tr", "tc", None))
    step = functools.partial(body, mesh.shape["tr"], mesh.shape["tc"])
    return jax.shard_map(step, mesh=mesh, in_specs=in_specs, out_specs=out_specs, check_vma=False)
```

```python
import functools
import math

import jax
import jax.numpy as jnp
from jax import lax
from jax.experimental import pallas as pl
from jax.experimental.pallas import tpu as pltpu
from jax.sharding import PartitionSpec as P

MESH = pl.DeviceIdType.MESH
FLAT = pl.DeviceIdType.LOGICAL
F32 = jnp.float32
BF16 = jnp.bfloat16


def dot_t(a, b):
    return lax.dot_general(a, b, (((1,), (1,)), ((), ())), preferred_element_type=F32)


def split(values):
    high = values.astype(BF16)
    low = (values - high.astype(F32)).astype(BF16)
    return high, low


def kernel(
    row_tiles, col_tiles, rows, cols,
    f1, f2, w1_hbm, w2_hbm, wp_hbm, bias_hbm,
    keys, query_out, offset_out,
    w1, w2, wp, bias,
    tiles, edge_rows, edge_out, edge_in,
    grid, patches, conv, hidden, patches2, conv2,
    pairs, stats, pool_a,
    in_sem, row_send, row_recv, edge_send, edge_recv, all_send, all_recv, key_recv, pair_send, pair_recv,
):
    tr = lax.axis_index("tr")
    tc = lax.axis_index("tc")
    devices = row_tiles * col_tiles
    me = tr * col_tiles + tc
    positions = float(devices * rows * cols)
    channels = wp.shape[1]
    pooled_cols = cols // 2

    loads = [
        pltpu.make_async_copy(f1, tiles.at[0], in_sem.at[0]),
        pltpu.make_async_copy(f2, tiles.at[1], in_sem.at[1]),
        pltpu.make_async_copy(w1_hbm, w1, in_sem.at[2]),
        pltpu.make_async_copy(w2_hbm, w2, in_sem.at[3]),
        pltpu.make_async_copy(wp_hbm, wp, in_sem.at[4]),
        pltpu.make_async_copy(bias_hbm, bias, in_sem.at[5]),
    ]
    for load in loads:
        load.start()

    edge_rows[...] = jnp.zeros_like(edge_rows)
    edge_in[...] = jnp.zeros_like(edge_in)

    def inside(down, side):
        row = tr + down
        col = tc + side
        return (row >= 0) & (row < row_tiles) & (col >= 0) & (col < col_tiles)

    far_first = sorted(range(1, devices), key=lambda s: -min(s, devices - s))
    close = (1, col_tiles - 1, col_tiles, col_tiles + 1)
    close_first = sorted(far_first, key=lambda s: min(s, devices - s) not in close)

    def wrap(index):
        return jnp.where(index < devices, index, index - devices)

    def each(act, order):
        def turn(step, carried=0):
            act(wrap(me + step))
            return carried

        if devices <= 32:
            for step in order:
                turn(step)
        else:
            lax.fori_loop(1, devices, turn, 0)

    barrier = pltpu.get_barrier_semaphore()

    def greet(index):
        pl.semaphore_signal(barrier, inc=1, device_id=index, device_id_type=FLAT)

    each(greet, close_first)

    loads[0].wait()
    loads[1].wait()
    left = 16
    right = left + cols
    for f in range(2):
        for y in range(2):
            values = tiles[f, y].astype(F32)
            grid[f, 2 + y, left:right, :] = values
            line = f * 4 + y * 2
            edge_out[0, line:line + 2, :] = values[0:2]
            edge_out[1, line:line + 2, :] = values[cols - 2:cols]

    pl.semaphore_wait(barrier, devices - 1)

    corners = [
        (0, 1, 1, 0), (0, -1, 0, 1),
        (1, 1, 1, 2), (1, -1, 0, 3),
        (-1, 1, 1, 4), (-1, -1, 0, 5),
    ]
    lines = [(1, 1, 0), (-1, 0, 1), (1, 0, 2), (-1, 1, 3)]

    def row_copy(f, down, row, slot):
        return pltpu.make_async_remote_copy(
            src_ref=tiles.at[f, row], dst_ref=edge_rows.at[slot, f],
            send_sem=row_send.at[slot, f], recv_sem=row_recv.at[slot, f],
            device_id=(tr + down, tc), device_id_type=MESH,
        )

    def edge_copy(down, side, which, slot):
        return pltpu.make_async_remote_copy(
            src_ref=edge_out.at[which], dst_ref=edge_in.at[slot],
            send_sem=edge_send.at[slot], recv_sem=edge_recv.at[slot],
            device_id=(tr + down, tc + side), device_id_type=MESH,
        )

    def send_row(f, line):
        @pl.when(inside(line[0], 0))
        def _():
            row_copy(f, *line).start()

    def send_edge(corner):
        @pl.when(inside(corner[0], corner[1]))
        def _():
            edge_copy(*corner).start()

    def await_row(f, line):
        landed = edge_rows.at[line[2], f]

        @pl.when(inside(-line[0], 0))
        def _():
            pltpu.make_async_copy(landed, landed, row_recv.at[line[2], f]).wait()

    def await_edge(corner):
        slot = corner[3]

        @pl.when(inside(-corner[0], -corner[1]))
        def _():
            pltpu.make_async_copy(edge_in.at[slot], edge_in.at[slot], edge_recv.at[slot]).wait()

    for corner in corners:
        send_edge(corner)
    for pair in (lines[:2], lines[2:]):
        for f in (1, 0):
            for line in pair:
                send_row(f, line)

    wide = cols + 16

    def fill_row(f, y, slot):
        grid[f, y, left:right, :] = edge_rows[slot, f].astype(F32)

    def fill_edges(f, y, slot, base):
        line = f * 4 + base * 2
        grid[f, y, left - 2:left, :] = edge_in[slot, line:line + 2, :]
        grid[f, y, right:right + 2, :] = edge_in[slot + 1, line:line + 2, :]

    def fill_patches(f, y):
        for j in range(3):
            start = left - 9 + j
            patches[f, y, :, j * 128:(j + 1) * 128] = grid[f, y, start:start + wide, :].astype(BF16)

    def patch(source, f, *lines_in):
        return jnp.concatenate([source[f, y] for y in lines_in], axis=1)

    def times(window, weights):
        return jnp.dot(window, weights, preferred_element_type=F32)

    def middle(weights):
        return jnp.concatenate([weights[384:1152], weights[0:768]], axis=1)

    core = lax.rem(tc, 2)
    sibling = jnp.where(core == 0, me + 1, me - 1)
    chips = devices // 2
    chip = me // 2
    far_chips = sorted(range(1, chips), key=lambda h: -min(h, chips - h))

    def each_chip(act, order):
        def turn(hop, carried=0):
            act(hop)
            return carried

        if chips <= 16:
            for hop in order:
                turn(hop)
        else:
            lax.fori_loop(1, chips, turn, 0)

    def share(upper, lower, phase):
        total = jnp.sum(upper + lower, axis=0, keepdims=True)
        squares = jnp.sum(upper * upper + lower * lower, axis=0, keepdims=True)
        pairs[phase, core] = jnp.concatenate([total, squares], axis=0)
        pltpu.make_async_remote_copy(
            src_ref=pairs.at[phase, core], dst_ref=pairs.at[phase, core],
            send_sem=pair_send.at[phase], recv_sem=pair_recv.at[phase],
            device_id=sibling, device_id_type=FLAT,
        ).start()

    def pass_on(phase):
        one = pairs.at[phase, 0]
        pltpu.make_async_copy(one, one, pair_recv.at[phase]).wait()
        stats[phase, chip] = pairs[phase, 0] + pairs[phase, 1]
        each_chip(lambda hop: pltpu.make_async_remote_copy(
            src_ref=stats.at[phase, chip], dst_ref=stats.at[phase, chip],
            send_sem=all_send.at[phase], recv_sem=all_recv.at[phase],
            device_id=wrap(me + 2 * hop), device_id_type=FLAT,
        ).start(), far_chips)

    def arrived(slots, sem):
        others = slots.at[pl.ds(0, chips - 1)]
        pltpu.make_async_copy(others, others, sem).wait()

    def collect(phase):
        arrived(stats.at[phase], all_recv.at[phase])
        total = jnp.sum(stats[phase], axis=0) / positions
        centre = total[0:1]
        spread = total[1:2] - centre * centre
        return centre, lax.rsqrt(spread + 1e-05)

    spot = lax.broadcasted_iota(jnp.int32, (wide, 128), 0)
    col_ok = ((spot >= 8) | (tc > 0)) & ((spot < 8 + cols) | (tc < col_tiles - 1))
    row_ok = (col_ok & (tr > 0), col_ok, col_ok, col_ok & (tr < row_tiles - 1))

    def start_own(f):
        for y in range(2):
            fill_edges(f, 2 + y, 0, y)
            fill_patches(f, 2 + y)
        return times(patch(patches, f, 2, 3), middle(w1))

    def finish_own(f, both):
        fill_row(f, 1, 0)
        fill_row(f, 4, 1)
        for y in range(2):
            fill_edges(f, 0 + y, 2, y)
            fill_edges(f, 4 + y, 4, y)
        fill_patches(f, 1)
        fill_patches(f, 4)
        conv[f, 1] = both[:, 0:128] + times(patches[f, 1], w1[0:384])
        conv[f, 2] = both[:, 128:256] + times(patches[f, 4], w1[768:1152])
        share(conv[f, 1, 8:8 + cols], conv[f, 2, 8:8 + cols], f)

    def edge_lines(f):
        fill_row(f, 0, 2)
        fill_row(f, 5, 3)
        fill_patches(f, 0)
        fill_patches(f, 5)
        conv[f, 0] = times(patch(patches, f, 0, 1, 2), w1[...])
        conv[f, 3] = times(patch(patches, f, 3, 4, 5), w1[...])

    def second_half(f):
        centre, inverse = collect(f)
        for y in range(4):
            values = jax.nn.relu((conv[f, y] - centre) * inverse)
            hidden[f, y, 8:8 + wide, :] = jnp.where(row_ok[y], values, 0.0)
            for j in range(3):
                start = left - 1 + j
                patches2[f, y, :, j * 128:(j + 1) * 128] = hidden[f, y, start:start + cols, :].astype(BF16)
        both = times(patch(patches2, f, 1, 2), middle(w2))
        upper = both[:, 0:128] + times(patches2[f, 0], w2[0:384])
        lower = both[:, 128:256] + times(patches2[f, 3], w2[768:1152])
        share(upper, lower, 2 + f)
        conv2[f, 0] = upper
        conv2[f, 1] = lower

    def blocks_of(f):
        centre, inverse = collect(2 + f)
        values = jax.nn.relu((conv2[f] - centre) * inverse)
        return jax.nn.relu(tiles[f].astype(F32) + values).astype(BF16)

    for corner in corners[:2]:
        await_edge(corner)
    loads[2].wait()
    both = start_own(1)
    for line in lines[:2]:
        await_row(1, line)
    for corner in corners[2:]:
        await_edge(corner)
    finish_own(1, both)
    both = start_own(0)
    pass_on(1)
    for line in lines[:2]:
        await_row(0, line)
    finish_own(0, both)
    for line in lines[2:]:
        await_row(1, line)
    edge_lines(1)
    pass_on(0)
    loads[3].wait()
    second_half(1)
    for line in lines[2:]:
        await_row(0, line)
    edge_lines(0)
    pass_on(3)
    second_half(0)
    pass_on(2)
    block = blocks_of(1)

    pool_a[0:cols, :] = block[0].astype(F32) + block[1].astype(F32)
    small = (pool_a[pl.ds(0, pooled_cols, stride=2), :] + pool_a[pl.ds(1, pooled_cols, stride=2), :]) * 0.25
    keys[me] = small.astype(BF16)
    def hand_over(block):
        pltpu.make_async_remote_copy(
            src_ref=keys.at[block], dst_ref=keys.at[block],
            send_sem=all_send.at[5], recv_sem=all_recv.at[5],
            device_id=sibling, device_id_type=FLAT,
        ).start()

    def send_key(hop):
        pltpu.make_async_remote_copy(
            src_ref=keys.at[me], dst_ref=keys.at[me],
            send_sem=all_send.at[4], recv_sem=key_recv.at[hop],
            device_id=wrap(me + 2 * hop), device_id_type=FLAT,
        ).start()

    def pass_key(hop):
        block = wrap(me + devices - 2 * hop)
        pltpu.make_async_copy(keys.at[block], keys.at[block], key_recv.at[hop]).wait()
        hand_over(block)

    each_chip(send_key, far_chips)
    hand_over(me)

    loads[4].wait()
    loads[5].wait()
    block = blocks_of(0)
    scale = 1.0 / math.sqrt(channels)
    feature = jnp.dot(block.reshape(2 * cols, 128), wp[...], preferred_element_type=F32) + bias[...]
    feature = feature.astype(BF16)
    offset = jnp.sum(feature.astype(F32) * bias[...], axis=1, keepdims=True) * scale
    high, low = split(dot_t(feature, wp[...]) * scale)
    queries = jnp.concatenate([high, low], axis=1)

    query_out[...] = queries
    offset_out[...] = jnp.broadcast_to(offset, offset_out.shape)

    each_chip(pass_key, far_chips[::-1])
    handed = keys.at[pl.ds(0, chips)]
    pltpu.make_async_copy(handed, handed, all_recv.at[5]).wait()

    for line in lines:
        for f in range(2):
            @pl.when(inside(line[0], 0))
            def _(slot=line[2], f=f):
                gone = edge_rows.at[slot, f]
                pltpu.make_async_copy(gone, gone, row_send.at[slot, f]).wait()

    for corner in corners:
        slot = corner[3]

        @pl.when(inside(corner[0], corner[1]))
        def _(slot=slot):
            pltpu.make_async_copy(edge_in.at[slot], edge_in.at[slot], edge_send.at[slot]).wait()

    for phase in range(4):
        arrived(stats.at[phase], all_send.at[phase])
        one = pairs.at[phase, 0]
        pltpu.make_async_copy(one, one, pair_send.at[phase]).wait()
    sent = keys.at[pl.ds(0, chips - 1)]
    pltpu.make_async_copy(sent, sent, all_send.at[4]).wait()
    pltpu.make_async_copy(handed, handed, all_send.at[5]).wait()


def correlate(across, keys, query, offset_ref, o1, o2, o3, pool_b, pool_c):
    total_keys = keys.shape[0]
    chunk = min(total_keys, 2048)
    lines1 = chunk // across
    queries = query[...]
    high = queries[:, 0:128]
    offset = offset_ref[:, 0:1]

    def pooled(values, scratch, lines_in, width):
        pairs = jnp.sum(values.reshape(lines_in // 2, 2, width, 128), axis=1)
        count = lines_in // 2 * width
        scratch[0:count, :] = pairs.reshape(count, 128)
        half = count // 2
        return (scratch[pl.ds(0, half, stride=2), :] + scratch[pl.ds(1, half, stride=2), :]) * 0.25

    def fine(values):
        k_high, k_low = split(values)
        return dot_t(queries, jnp.concatenate([k_high, k_high], axis=1)) + dot_t(high, k_low) + offset

    for start in range(0, total_keys, chunk):
        part = keys[start:start + chunk, :]
        level = dot_t(queries, jnp.concatenate([part, part], axis=1)) + offset
        o1[:, start:start + chunk] = level.astype(BF16)
        two = pooled(part.astype(F32), pool_b, lines1, across)
        o2[:, start // 4:(start + chunk) // 4] = fine(two).astype(BF16)
        three = pooled(two, pool_c, lines1 // 2, across // 2)
        o3[:, start // 16:(start + chunk) // 16] = fine(three).astype(BF16)


def body(row_tiles, col_tiles, frame_one, frame_two, first_kernel, second_kernel, out_proj, out_bias):
    rows, cols, cin = frame_one.shape
    channels = out_proj.shape[1]
    devices = row_tiles * col_tiles
    queries = rows * cols
    keys = devices * queries // 4
    wide = cols + 16
    chunk = min(keys, 2048)
    vmem = pltpu.VMEM
    anywhere = pl.BlockSpec(memory_space=pl.ANY)
    local = pl.BlockSpec(memory_space=pltpu.VMEM)
    key_blocks, query, offset = pl.pallas_call(
        functools.partial(kernel, row_tiles, col_tiles, rows, cols),
        out_shape=[
            jax.ShapeDtypeStruct((devices, cols // 2, cin), BF16),
            jax.ShapeDtypeStruct((queries, 2 * cin), BF16),
            jax.ShapeDtypeStruct((queries, 128), F32),
        ],
        in_specs=[anywhere] * 6,
        out_specs=[local] * 3,
        scratch_shapes=[
            vmem((9 * cin, cin), BF16),
            vmem((9 * cin, cin), BF16),
            vmem((cin, channels), BF16),
            vmem((1, channels), F32),
            vmem((2, rows, cols, cin), BF16),
            vmem((4, 2, cols, cin), BF16),
            vmem((2, 8, cin), F32),
            vmem((6, 8, cin), F32),
            vmem((2, 6, cols + 32, cin), F32),
            vmem((2, 6, wide, 3 * cin), BF16),
            vmem((2, 4, wide, cin), F32),
            vmem((2, 4, cols + 32, cin), F32),
            vmem((2, 4, cols, 3 * cin), BF16),
            vmem((2, rows, cols, cin), F32),
            vmem((4, 2, 2, cin), F32),
            vmem((4, devices // 2, 2, cin), F32),
            vmem((cols, cin), F32),
            pltpu.SemaphoreType.DMA((6,)),
            pltpu.SemaphoreType.DMA((4, 2)),
            pltpu.SemaphoreType.DMA((4, 2)),
            pltpu.SemaphoreType.DMA((6,)),
            pltpu.SemaphoreType.DMA((6,)),
            pltpu.SemaphoreType.DMA((6,)),
            pltpu.SemaphoreType.DMA((6,)),
            pltpu.SemaphoreType.DMA((devices // 2,)),
            pltpu.SemaphoreType.DMA((4,)),
            pltpu.SemaphoreType.DMA((4,)),
        ],
        compiler_params=pltpu.CompilerParams(
            collective_id=0, has_side_effects=True, vmem_limit_bytes=48 * 1024 * 1024
        ),
    )(*[
        pltpu.with_memory_space_constraint(value, pltpu.HBM)
        for value in (
            frame_one, frame_two,
            first_kernel.reshape(9 * cin, cin), second_kernel.reshape(9 * cin, cin),
            out_proj, out_bias.reshape(1, channels),
        )
    ])
    outs = pl.pallas_call(
        functools.partial(correlate, col_tiles * cols // 2),
        out_shape=[
            jax.ShapeDtypeStruct((queries, keys), BF16),
            jax.ShapeDtypeStruct((queries, keys // 4), BF16),
            jax.ShapeDtypeStruct((queries, keys // 16), BF16),
        ],
        in_specs=[local] * 3,
        out_specs=[local] * 3,
        scratch_shapes=[vmem((chunk // 2, cin), F32), vmem((chunk // 8, cin), F32)],
        compiler_params=pltpu.CompilerParams(vmem_limit_bytes=24 * 1024 * 1024),
    )(key_blocks.reshape(keys, cin), query, offset)
    return tuple(out.reshape(rows, cols, -1) for out in outs)


def solution(mesh):
    in_specs = (P("tr", "tc", None), P("tr", "tc", None), P(), P(), P(), P())
    out_specs = (P("tr", "tc", None), P("tr", "tc", None), P("tr", "tc", None))
    step = functools.partial(body, mesh.shape["tr"], mesh.shape["tc"])
    return jax.shard_map(step, mesh=mesh, in_specs=in_specs, out_specs=out_specs, check_vma=False)
```

```python
import functools
import math

import jax
import jax.numpy as jnp
from jax import lax
from jax.experimental import pallas as pl
from jax.experimental.pallas import tpu as pltpu
from jax.sharding import PartitionSpec as P

MESH = pl.DeviceIdType.MESH
FLAT = pl.DeviceIdType.LOGICAL
F32 = jnp.float32
BF16 = jnp.bfloat16


def dot_t(a, b):
    return lax.dot_general(a, b, (((1,), (1,)), ((), ())), preferred_element_type=F32)


def split(values):
    high = values.astype(BF16)
    low = (values - high.astype(F32)).astype(BF16)
    return high, low


def kernel(
    row_tiles, col_tiles, rows, cols,
    f1, f2, w1_hbm, w2_hbm, wp_hbm, bias_hbm,
    keys, query_out, offset_out,
    w1, w2, wp, bias,
    tiles, edge_rows, edge_out, edge_in,
    grid, patches, conv, hidden, patches2, conv2,
    stats, pool_a,
    in_sem, row_send, row_recv, edge_send, edge_recv, all_send, all_recv, key_recv,
):
    tr = lax.axis_index("tr")
    tc = lax.axis_index("tc")
    devices = row_tiles * col_tiles
    me = tr * col_tiles + tc
    positions = float(devices * rows * cols)
    channels = wp.shape[1]
    pooled_cols = cols // 2

    loads = [
        pltpu.make_async_copy(f1, tiles.at[0], in_sem.at[0]),
        pltpu.make_async_copy(f2, tiles.at[1], in_sem.at[1]),
        pltpu.make_async_copy(w1_hbm, w1, in_sem.at[2]),
        pltpu.make_async_copy(w2_hbm, w2, in_sem.at[3]),
        pltpu.make_async_copy(wp_hbm, wp, in_sem.at[4]),
        pltpu.make_async_copy(bias_hbm, bias, in_sem.at[5]),
    ]
    for load in loads:
        load.start()

    edge_rows[...] = jnp.zeros_like(edge_rows)
    edge_in[...] = jnp.zeros_like(edge_in)

    def inside(down, side):
        row = tr + down
        col = tc + side
        return (row >= 0) & (row < row_tiles) & (col >= 0) & (col < col_tiles)

    far_first = sorted(range(1, devices), key=lambda s: -min(s, devices - s))
    close = (1, col_tiles - 1, col_tiles, col_tiles + 1)
    close_first = sorted(far_first, key=lambda s: min(s, devices - s) not in close)

    def wrap(index):
        return jnp.where(index < devices, index, index - devices)

    def each(act, order):
        def turn(step, carried=0):
            act(wrap(me + step))
            return carried

        if devices <= 32:
            for step in order:
                turn(step)
        else:
            lax.fori_loop(1, devices, turn, 0)

    barrier = pltpu.get_barrier_semaphore()

    def greet(index):
        pl.semaphore_signal(barrier, inc=1, device_id=index, device_id_type=FLAT)

    each(greet, close_first)

    loads[0].wait()
    loads[1].wait()
    left = 16
    right = left + cols
    for f in range(2):
        for y in range(2):
            values = tiles[f, y].astype(F32)
            grid[f, 2 + y, left:right, :] = values
            line = f * 4 + y * 2
            edge_out[0, line:line + 2, :] = values[0:2]
            edge_out[1, line:line + 2, :] = values[cols - 2:cols]

    pl.semaphore_wait(barrier, devices - 1)

    corners = [
        (0, 1, 1, 0), (0, -1, 0, 1),
        (1, 1, 1, 2), (1, -1, 0, 3),
        (-1, 1, 1, 4), (-1, -1, 0, 5),
    ]
    lines = [(1, 1, 0), (-1, 0, 1), (1, 0, 2), (-1, 1, 3)]

    def row_copy(f, down, row, slot):
        return pltpu.make_async_remote_copy(
            src_ref=tiles.at[f, row], dst_ref=edge_rows.at[slot, f],
            send_sem=row_send.at[slot, f], recv_sem=row_recv.at[slot, f],
            device_id=(tr + down, tc), device_id_type=MESH,
        )

    def edge_copy(down, side, which, slot):
        return pltpu.make_async_remote_copy(
            src_ref=edge_out.at[which], dst_ref=edge_in.at[slot],
            send_sem=edge_send.at[slot], recv_sem=edge_recv.at[slot],
            device_id=(tr + down, tc + side), device_id_type=MESH,
        )

    def send_row(f, line):
        @pl.when(inside(line[0], 0))
        def _():
            row_copy(f, *line).start()

    def send_edge(corner):
        @pl.when(inside(corner[0], corner[1]))
        def _():
            edge_copy(*corner).start()

    def await_row(f, line):
        landed = edge_rows.at[line[2], f]

        @pl.when(inside(-line[0], 0))
        def _():
            pltpu.make_async_copy(landed, landed, row_recv.at[line[2], f]).wait()

    def await_edge(corner):
        slot = corner[3]

        @pl.when(inside(-corner[0], -corner[1]))
        def _():
            pltpu.make_async_copy(edge_in.at[slot], edge_in.at[slot], edge_recv.at[slot]).wait()

    for corner in corners:
        send_edge(corner)
    for line in lines:
        send_row(1, line)

    wide = cols + 16

    def fill_row(f, y, slot):
        grid[f, y, left:right, :] = edge_rows[slot, f].astype(F32)

    def fill_edges(f, y, slot, base):
        line = f * 4 + base * 2
        grid[f, y, left - 2:left, :] = edge_in[slot, line:line + 2, :]
        grid[f, y, right:right + 2, :] = edge_in[slot + 1, line:line + 2, :]

    def fill_patches(f, y):
        for j in range(3):
            start = left - 9 + j
            patches[f, y, :, j * 128:(j + 1) * 128] = grid[f, y, start:start + wide, :].astype(BF16)

    def patch(source, f, *lines_in):
        return jnp.concatenate([source[f, y] for y in lines_in], axis=1)

    def times(window, weights):
        return jnp.dot(window, weights, preferred_element_type=F32)

    def middle(weights):
        return jnp.concatenate([weights[384:1152], weights[0:768]], axis=1)

    def send_block(slots, phase):
        each(lambda index: pltpu.make_async_remote_copy(
            src_ref=slots.at[me], dst_ref=slots.at[me],
            send_sem=all_send.at[phase], recv_sem=all_recv.at[phase],
            device_id=index, device_id_type=FLAT,
        ).start(), far_first)

    def arrived(slots, sem):
        others = slots.at[pl.ds(0, devices - 1)]
        pltpu.make_async_copy(others, others, sem).wait()

    def share(upper, lower, phase):
        total = jnp.sum(upper + lower, axis=0, keepdims=True)
        squares = jnp.sum(upper * upper + lower * lower, axis=0, keepdims=True)
        stats[phase, me] = jnp.concatenate([total, squares], axis=0)
        send_block(stats.at[phase], phase)

    def collect(phase):
        arrived(stats.at[phase], all_recv.at[phase])
        total = jnp.sum(stats[phase], axis=0) / positions
        centre = total[0:1]
        spread = total[1:2] - centre * centre
        return centre, lax.rsqrt(spread + 1e-05)

    spot = lax.broadcasted_iota(jnp.int32, (wide, 128), 0)
    col_ok = ((spot >= 8) | (tc > 0)) & ((spot < 8 + cols) | (tc < col_tiles - 1))
    row_ok = (col_ok & (tr > 0), col_ok, col_ok, col_ok & (tr < row_tiles - 1))

    def start_own(f):
        for y in range(2):
            fill_edges(f, 2 + y, 0, y)
            fill_patches(f, 2 + y)
        return times(patch(patches, f, 2, 3), middle(w1))

    def finish_own(f, both):
        fill_row(f, 1, 0)
        fill_row(f, 4, 1)
        for y in range(2):
            fill_edges(f, 0 + y, 2, y)
            fill_edges(f, 4 + y, 4, y)
        fill_patches(f, 1)
        fill_patches(f, 4)
        conv[f, 1] = both[:, 0:128] + times(patches[f, 1], w1[0:384])
        conv[f, 2] = both[:, 128:256] + times(patches[f, 4], w1[768:1152])
        share(conv[f, 1, 8:8 + cols], conv[f, 2, 8:8 + cols], f)

    def edge_lines(f):
        fill_row(f, 0, 2)
        fill_row(f, 5, 3)
        fill_patches(f, 0)
        fill_patches(f, 5)
        conv[f, 0] = times(patch(patches, f, 0, 1, 2), w1[...])
        conv[f, 3] = times(patch(patches, f, 3, 4, 5), w1[...])

    def second_half(f):
        centre, inverse = collect(f)
        for y in range(4):
            values = jax.nn.relu((conv[f, y] - centre) * inverse)
            hidden[f, y, 8:8 + wide, :] = jnp.where(row_ok[y], values, 0.0)
            for j in range(3):
                start = left - 1 + j
                patches2[f, y, :, j * 128:(j + 1) * 128] = hidden[f, y, start:start + cols, :].astype(BF16)
        both = times(patch(patches2, f, 1, 2), middle(w2))
        upper = both[:, 0:128] + times(patches2[f, 0], w2[0:384])
        lower = both[:, 128:256] + times(patches2[f, 3], w2[768:1152])
        share(upper, lower, 2 + f)
        conv2[f, 0] = upper
        conv2[f, 1] = lower

    def blocks_of(f):
        centre, inverse = collect(2 + f)
        values = jax.nn.relu((conv2[f] - centre) * inverse)
        return jax.nn.relu(tiles[f].astype(F32) + values).astype(BF16)

    for corner in corners[:2]:
        await_edge(corner)
    loads[2].wait()
    both = start_own(1)
    for line in lines[:2]:
        await_row(1, line)
    for corner in corners[2:]:
        await_edge(corner)
    finish_own(1, both)
    for line in lines:
        send_row(0, line)
    both = start_own(0)
    for line in lines[2:]:
        await_row(1, line)
    edge_lines(1)
    loads[3].wait()
    second_half(1)
    for line in lines[:2]:
        await_row(0, line)
    finish_own(0, both)
    for line in lines[2:]:
        await_row(0, line)
    edge_lines(0)
    block = blocks_of(1)

    pool_a[0:cols, :] = block[0].astype(F32) + block[1].astype(F32)
    small = (pool_a[pl.ds(0, pooled_cols, stride=2), :] + pool_a[pl.ds(1, pooled_cols, stride=2), :]) * 0.25
    keys[me] = small.astype(BF16)
    sibling = jnp.where(lax.rem(tc, 2) == 0, me + 1, me - 1)
    chips = devices // 2

    def hand_over(block):
        pltpu.make_async_remote_copy(
            src_ref=keys.at[block], dst_ref=keys.at[block],
            send_sem=all_send.at[5], recv_sem=all_recv.at[5],
            device_id=sibling, device_id_type=FLAT,
        ).start()

    def send_key(hop):
        pltpu.make_async_remote_copy(
            src_ref=keys.at[me], dst_ref=keys.at[me],
            send_sem=all_send.at[4], recv_sem=key_recv.at[hop],
            device_id=wrap(me + 2 * hop), device_id_type=FLAT,
        ).start()

    def pass_key(hop):
        block = wrap(me + devices - 2 * hop)
        pltpu.make_async_copy(keys.at[block], keys.at[block], key_recv.at[hop]).wait()
        hand_over(block)

    def each_chip(act, order):
        def turn(hop, carried=0):
            act(hop)
            return carried

        if chips <= 16:
            for hop in order:
                turn(hop)
        else:
            lax.fori_loop(1, chips, turn, 0)

    far_chips = sorted(range(1, chips), key=lambda h: -min(h, chips - h))
    each_chip(send_key, far_chips)
    hand_over(me)
    second_half(0)

    loads[4].wait()
    loads[5].wait()
    block = blocks_of(0)
    scale = 1.0 / math.sqrt(channels)
    feature = jnp.dot(block.reshape(2 * cols, 128), wp[...], preferred_element_type=F32) + bias[...]
    feature = feature.astype(BF16)
    offset = jnp.sum(feature.astype(F32) * bias[...], axis=1, keepdims=True) * scale
    high, low = split(dot_t(feature, wp[...]) * scale)
    queries = jnp.concatenate([high, low], axis=1)

    query_out[...] = queries
    offset_out[...] = jnp.broadcast_to(offset, offset_out.shape)

    each_chip(pass_key, far_chips[::-1])
    handed = keys.at[pl.ds(0, chips)]
    pltpu.make_async_copy(handed, handed, all_recv.at[5]).wait()

    for line in lines:
        for f in range(2):
            @pl.when(inside(line[0], 0))
            def _(slot=line[2], f=f):
                gone = edge_rows.at[slot, f]
                pltpu.make_async_copy(gone, gone, row_send.at[slot, f]).wait()

    for corner in corners:
        slot = corner[3]

        @pl.when(inside(corner[0], corner[1]))
        def _(slot=slot):
            pltpu.make_async_copy(edge_in.at[slot], edge_in.at[slot], edge_send.at[slot]).wait()

    for phase in range(4):
        arrived(stats.at[phase], all_send.at[phase])
    sent = keys.at[pl.ds(0, chips - 1)]
    pltpu.make_async_copy(sent, sent, all_send.at[4]).wait()
    pltpu.make_async_copy(handed, handed, all_send.at[5]).wait()


def correlate(across, keys, query, offset_ref, o1, o2, o3, pool_b, pool_c):
    total_keys = keys.shape[0]
    chunk = min(total_keys, 2048)
    lines1 = chunk // across
    queries = query[...]
    high = queries[:, 0:128]
    offset = offset_ref[:, 0:1]

    def pooled(values, scratch, lines_in, width):
        pairs = jnp.sum(values.reshape(lines_in // 2, 2, width, 128), axis=1)
        count = lines_in // 2 * width
        scratch[0:count, :] = pairs.reshape(count, 128)
        half = count // 2
        return (scratch[pl.ds(0, half, stride=2), :] + scratch[pl.ds(1, half, stride=2), :]) * 0.25

    def fine(values):
        k_high, k_low = split(values)
        return dot_t(queries, jnp.concatenate([k_high, k_high], axis=1)) + dot_t(high, k_low) + offset

    for start in range(0, total_keys, chunk):
        part = keys[start:start + chunk, :]
        level = dot_t(queries, jnp.concatenate([part, part], axis=1)) + offset
        o1[:, start:start + chunk] = level.astype(BF16)
        two = pooled(part.astype(F32), pool_b, lines1, across)
        o2[:, start // 4:(start + chunk) // 4] = fine(two).astype(BF16)
        three = pooled(two, pool_c, lines1 // 2, across // 2)
        o3[:, start // 16:(start + chunk) // 16] = fine(three).astype(BF16)


def body(row_tiles, col_tiles, frame_one, frame_two, first_kernel, second_kernel, out_proj, out_bias):
    rows, cols, cin = frame_one.shape
    channels = out_proj.shape[1]
    devices = row_tiles * col_tiles
    queries = rows * cols
    keys = devices * queries // 4
    wide = cols + 16
    chunk = min(keys, 2048)
    vmem = pltpu.VMEM
    anywhere = pl.BlockSpec(memory_space=pl.ANY)
    local = pl.BlockSpec(memory_space=pltpu.VMEM)
    key_blocks, query, offset = pl.pallas_call(
        functools.partial(kernel, row_tiles, col_tiles, rows, cols),
        out_shape=[
            jax.ShapeDtypeStruct((devices, cols // 2, cin), BF16),
            jax.ShapeDtypeStruct((queries, 2 * cin), BF16),
            jax.ShapeDtypeStruct((queries, 128), F32),
        ],
        in_specs=[anywhere] * 6,
        out_specs=[local] * 3,
        scratch_shapes=[
            vmem((9 * cin, cin), BF16),
            vmem((9 * cin, cin), BF16),
            vmem((cin, channels), BF16),
            vmem((1, channels), F32),
            vmem((2, rows, cols, cin), BF16),
            vmem((4, 2, cols, cin), BF16),
            vmem((2, 8, cin), F32),
            vmem((6, 8, cin), F32),
            vmem((2, 6, cols + 32, cin), F32),
            vmem((2, 6, wide, 3 * cin), BF16),
            vmem((2, 4, wide, cin), F32),
            vmem((2, 4, cols + 32, cin), F32),
            vmem((2, 4, cols, 3 * cin), BF16),
            vmem((2, rows, cols, cin), F32),
            vmem((4, devices, 2, cin), F32),
            vmem((cols, cin), F32),
            pltpu.SemaphoreType.DMA((6,)),
            pltpu.SemaphoreType.DMA((4, 2)),
            pltpu.SemaphoreType.DMA((4, 2)),
            pltpu.SemaphoreType.DMA((6,)),
            pltpu.SemaphoreType.DMA((6,)),
            pltpu.SemaphoreType.DMA((6,)),
            pltpu.SemaphoreType.DMA((6,)),
            pltpu.SemaphoreType.DMA((devices // 2,)),
        ],
        compiler_params=pltpu.CompilerParams(
            collective_id=0, has_side_effects=True, vmem_limit_bytes=48 * 1024 * 1024
        ),
    )(*[
        pltpu.with_memory_space_constraint(value, pltpu.HBM)
        for value in (
            frame_one, frame_two,
            first_kernel.reshape(9 * cin, cin), second_kernel.reshape(9 * cin, cin),
            out_proj, out_bias.reshape(1, channels),
        )
    ])
    outs = pl.pallas_call(
        functools.partial(correlate, col_tiles * cols // 2),
        out_shape=[
            jax.ShapeDtypeStruct((queries, keys), BF16),
            jax.ShapeDtypeStruct((queries, keys // 4), BF16),
            jax.ShapeDtypeStruct((queries, keys // 16), BF16),
        ],
        in_specs=[local] * 3,
        out_specs=[local] * 3,
        scratch_shapes=[vmem((chunk // 2, cin), F32), vmem((chunk // 8, cin), F32)],
        compiler_params=pltpu.CompilerParams(vmem_limit_bytes=24 * 1024 * 1024),
    )(key_blocks.reshape(keys, cin), query, offset)
    return tuple(out.reshape(rows, cols, -1) for out in outs)


def solution(mesh):
    in_specs = (P("tr", "tc", None), P("tr", "tc", None), P(), P(), P(), P())
    out_specs = (P("tr", "tc", None), P("tr", "tc", None), P("tr", "tc", None))
    step = functools.partial(body, mesh.shape["tr"], mesh.shape["tc"])
    return jax.shard_map(step, mesh=mesh, in_specs=in_specs, out_specs=out_specs, check_vma=False)
```
